32 devices in a mesh: wide: 8 (over z, core), narrow: 4 (over y, x).
Axes of the slice: x: 2, y: 2, z: 4, core: 2. Of those that a mesh axis runs over, the one named last changes fastest.
Arguments:
- fields: float32 [5, 8, 32, 256], P(None, 'wide', 'narrow'), may hold values from -2.1 to 6.1, as said below
- prior_modes: bfloat16 [124, 5, 8, 8192], P(None, None, 'wide', 'narrow'), may hold values from -360 to 360, as said below
Outputs:
- flow_state: float32 [5, 8, 32, 256], P(None, 'wide', 'narrow')
- factor: float32 [128, 128], replicated
The draws below stay inside these ranges and needn't reach their ends.
Inputs may be any that keep to these rules, and one draw needn't show every extreme that they name: `fields`: density and pressure lie in 0.6 to 1.4, each velocity component below 1.5 in magnitude. `prior_modes`: the columns are linearly independent.
All inputs are finite; a program needn't handle non-finite values.
Results may differ from the reference program's by a relative error of at most 0.0014.
Values may be sent and summed in bfloat16 or wider, within the bound.
A program may use at most 64 MiB of HBM per device.

```python
import jax
import jax.numpy as jnp
from jax import lax

COLS = 128
SNAPS = 4
STEPS = 2
PRIOR = 124
NX = 8
NY = 32
NZ = 256


GAMMA = 1.4


def base_state(key):
    key_density, key_velocity, key_pressure = jax.random.split(jax.random.fold_in(key, 101), 3)
    density = jax.random.uniform(key_density, (NX, NY, NZ), jnp.float32, 0.6, 1.4)
    velocity = 0.3 * jax.random.truncated_normal(key_velocity, -3.0, 3.0, (3, NX, NY, NZ), jnp.float32)
    pressure = jax.random.uniform(key_pressure, (NX, NY, NZ), jnp.float32, 0.6, 1.4)
    momentum = density[None] * velocity
    energy = pressure / (GAMMA - 1.0) + 0.5 * density * jnp.sum(velocity * velocity, 0)
    return jnp.concatenate([density[None], momentum, energy[None]], 0)


def bump_profile(key, length_cells):
    spread = length_cells / 8.0
    centre = jax.random.uniform(key, (PRIOR,), jnp.float32, 0.0, 1.0) * length_cells
    position = jnp.arange(length_cells, dtype=jnp.float32) + 0.5
    distance = jnp.abs(position[None, :] - centre[:, None])
    distance = jnp.minimum(distance, length_cells - distance)
    scaled = distance / spread
    return jnp.exp(-0.5 * scaled * scaled)


def draw_fields(key, part):
    return base_state(key)


def draw_prior_modes(key, part):
    state_base = jnp.swapaxes(base_state(key), 2, 3)
    coefficients = jax.random.uniform(jax.random.fold_in(key, 202), (PRIOR,), jnp.float32, -1.0, 1.0)
    scales = jnp.exp(jax.random.uniform(jax.random.fold_in(key, 212), (PRIOR,), jnp.float32, jnp.log(0.2), jnp.log(2.0)))
    bump_x = bump_profile(jax.random.fold_in(key, 222), NX)
    bump_y = bump_profile(jax.random.fold_in(key, 232), NY)
    bump_z = bump_profile(jax.random.fold_in(key, 242), NZ)
    envelope = 1.0 + 7.0 * bump_x[:, :, None, None] * bump_z[:, None, :, None] * bump_y[:, None, None, :]
    disorder = jax.random.truncated_normal(jax.random.fold_in(key, 303), -4.0, 4.0, (PRIOR, 5, NX, NZ, NY), jnp.float32)
    columns_all = scales[:, None, None, None, None] * envelope[:, None] * (coefficients[:, None, None, None, None] * state_base[None] + disorder)
    return columns_all.reshape(PRIOR, 5, NX, NZ * NY).astype(jnp.bfloat16)


def setup_inputs(seed: int = 0) -> dict:
    seeds = jax.random.split(jax.random.key(seed), 3)
    return {
        "fields": draw_fields(jax.random.fold_in(seeds[2], 71), 0),
        "prior_modes": draw_prior_modes(jax.random.fold_in(seeds[2], 71), 0),
    }


GAMMA = 1.4
TIME_STEP = 0.25
VISCOSITY = 0.15

def flux_of(current, dim_index):
    density = current[0]
    momentum = current[1:4]
    energy = current[4]
    vel_d = momentum[dim_index] / density
    pressure = (GAMMA - 1.0) * (energy - 0.5 * (momentum[0] * momentum[0] + momentum[1] * momentum[1] + momentum[2] * momentum[2]) / density)
    components = [momentum[dim_index], momentum[0] * vel_d, momentum[1] * vel_d, momentum[2] * vel_d, (energy + pressure) * vel_d]
    components[1 + dim_index] = components[1 + dim_index] + pressure
    return jnp.stack(components)

def tendency(current):
    flux_x = flux_of(current, 0)
    flux_y = flux_of(current, 1)
    flux_z = flux_of(current, 2)
    divergence = jnp.roll(flux_x, -1, 1) - jnp.roll(flux_x, 1, 1) + (jnp.roll(flux_y, -1, 2) - jnp.roll(flux_y, 1, 2)) + (jnp.roll(flux_z, -1, 3) - jnp.roll(flux_z, 1, 3))
    laplace = jnp.roll(current, -1, 1) + jnp.roll(current, 1, 1) + jnp.roll(current, -1, 2) + jnp.roll(current, 1, 2) + jnp.roll(current, -1, 3) + jnp.roll(current, 1, 3) - 6.0 * current
    return -0.5 * divergence + VISCOSITY * laplace

def reference(fields, prior_modes):
    current = fields
    snapshots = []
    for step_index in range(STEPS):
        section_one = current + TIME_STEP * tendency(current)
        snapshots.append(section_one.astype(jnp.bfloat16))
        current = 0.5 * current + 0.5 * (section_one + TIME_STEP * tendency(section_one))
        snapshots.append(current.astype(jnp.bfloat16))
    snap_stack = jnp.swapaxes(jnp.stack(snapshots), 3, 4).reshape(SNAPS, 5, NX, NZ * NY)

    def accumulate(x_index, gram_total):
        basis_rows = lax.dynamic_index_in_dim(prior_modes, x_index, 2, keepdims=False).reshape(PRIOR, -1).astype(jnp.float32)
        snap_rows = lax.dynamic_index_in_dim(snap_stack, x_index, 2, keepdims=False).reshape(SNAPS, -1).astype(jnp.float32)
        stacked = jnp.concatenate([basis_rows, snap_rows], 0)
        return gram_total + jnp.dot(stacked, stacked.T, precision=lax.Precision.HIGHEST)
    gram_total = lax.fori_loop(0, NX, accumulate, jnp.zeros((COLS, COLS), jnp.float32))
    gram_total = gram_total * (1.0 / (NX * NY * NZ))
    factor = jnp.linalg.cholesky(gram_total).T
    return (current, factor)
```

```python
import functools

import jax
import jax.numpy as jnp
from jax import lax
from jax.experimental import pallas as pl
from jax.experimental.pallas import tpu as pltpu
from jax.sharding import PartitionSpec as P

STEPS = 2
GAMMA = 1.4
TIME_STEP = 0.25
VISCOSITY = 0.15
LANES = 128
NT = (((1,), (1,)), ((), ()))


def flux_of(state, d):
    density, energy = state[0], state[4]
    momentum = state[1:4]
    inverse = 1.0 / density
    vel = momentum[d] * inverse
    squares = momentum[0] * momentum[0] + momentum[1] * momentum[1] + momentum[2] * momentum[2]
    pressure = (GAMMA - 1.0) * (energy - 0.5 * squares * inverse)
    out = [momentum[d], momentum[0] * vel, momentum[1] * vel, momentum[2] * vel]
    out.append((energy + pressure) * vel)
    out[1 + d] = out[1 + d] + pressure
    return out


def tendency(here, x_low, x_high, y_low, y_high):
    cells_z = here[0].shape[1]
    z_low = [pltpu.roll(c, 1, 1) for c in here]
    z_high = [pltpu.roll(c, cells_z - 1, 1) for c in here]
    total = None
    for d, (low, high) in enumerate(((x_low, x_high), (y_low, y_high), (z_low, z_high))):
        flux_low, flux_high = flux_of(low, d), flux_of(high, d)
        part = [
            -0.5 * (fh - fl) + VISCOSITY * (l + h)
            for fh, fl, l, h in zip(flux_high, flux_low, low, high)
        ]
        total = part if total is None else [a + b for a, b in zip(total, part)]
    return [t - (6.0 * VISCOSITY) * c for t, c in zip(total, here)]


def eliminate(tiles, size):
    row_id = lax.broadcasted_iota(jnp.int32, (8, LANES), 0)
    done = []
    tiles = list(tiles)
    for p in range(size // 8):
        scale = jnp.zeros((8, LANES), jnp.float32)
        for k in range(8):
            j = 8 * p + k
            column = jnp.broadcast_to(tiles[p][:, j : j + 1], (8, LANES))
            pivot = jnp.broadcast_to(column[k : k + 1, :], (8, LANES))
            row = jnp.broadcast_to(tiles[p][k : k + 1, :], (8, LANES))
            row = row / pivot
            scale = jnp.where(row_id == k, pivot, scale)
            tiles[p] = tiles[p] - jnp.where(row_id > k, column, 0.0) * row
            for t in range(p + 1, size // 8):
                tiles[t] = tiles[t] - jnp.broadcast_to(tiles[t][:, j : j + 1], (8, LANES)) * row
        lane = lax.broadcasted_iota(jnp.int32, (8, LANES), 1)
        done.append(jnp.where(lane >= row_id + 8 * p, tiles[p] * lax.rsqrt(scale), 0.0))
    return done


def factor_kernel(gram_ref, out_ref):
    size = gram_ref.shape[0]
    tiles = [gram_ref[8 * t : 8 * t + 8, :] for t in range(size // 8)]
    for t, rows in enumerate(eliminate(tiles, size)):
        out_ref[8 * t : 8 * t + 8, :] = rows


def kernel(
    wide, narrow, fields, modes_hbm, flow, gram_out,
    modes, modes_sem, state, x_halo, y_send, y_halo, halo_send, halo_recv,
    snap_out, snap_in, snap_send, snap_recv,
    gram, scatter, part, share, whole, piece, red_send, red_recv,
    tail, rows8, rows_n, sums8, rows_w, last_send, last_recv,
):
    stages = 2 * STEPS
    comps, cells_y, cells_z = fields.shape
    prior = modes.shape[1]
    columns = gram.shape[0]
    mode_lanes = modes.shape[2]
    y_all = cells_y * narrow
    z_own = cells_z // narrow
    z_group = LANES // y_all
    groups = mode_lanes // LANES
    piece_rows = columns // wide
    keep = columns - 16
    iw, jn = lax.axis_index("wide"), lax.axis_index("narrow")

    def w_peer(d):
        return lax.rem(iw + d, wide)

    def n_peer(d):
        return lax.rem(jn + d, narrow)

    def remote(src, dst, send, recv, device):
        return pltpu.make_async_remote_copy(
            src_ref=src, dst_ref=dst, send_sem=send, recv_sem=recv,
            device_id=device, device_id_type=pl.DeviceIdType.MESH,
        )

    loads = [pltpu.make_async_copy(modes_hbm.at[c], modes.at[c], modes_sem.at[c]) for c in range(comps)]
    for load in loads:
        load.start()

    barrier = pltpu.get_barrier_semaphore()
    for d in range(1, wide):
        pl.semaphore_signal(barrier, inc=1, device_id=(w_peer(d), jn), device_id_type=pl.DeviceIdType.MESH)
    for d in range(1, narrow):
        pl.semaphore_signal(barrier, inc=1, device_id=(iw, n_peer(d)), device_id_type=pl.DeviceIdType.MESH)

    def halo_copies(s):
        right, left = (w_peer(1), jn), (w_peer(wide - 1), jn)
        up, down = (iw, n_peer(1)), (iw, n_peer(narrow - 1))
        return [
            remote(state.at[s], x_halo.at[s, 0], halo_send.at[s, 0], halo_recv.at[s, 0], right),
            remote(state.at[s], x_halo.at[s, 1], halo_send.at[s, 1], halo_recv.at[s, 1], left),
            remote(y_send.at[s, 1], y_halo.at[s, 0], halo_send.at[s, 2], halo_recv.at[s, 2], up),
            remote(y_send.at[s, 0], y_halo.at[s, 1], halo_send.at[s, 3], halo_recv.at[s, 3], down),
        ]

    def put_state(s, values):
        for c in range(comps):
            state[s, c] = values[c]
            y_send[s, 0, c : c + 1, :] = values[c][0:1, :]
            y_send[s, 1, c : c + 1, :] = values[c][cells_y - 1 : cells_y, :]
        for c in range(comps, 8):
            y_send[s, 0, c : c + 1, :] = jnp.zeros((1, cells_z), jnp.float32)
            y_send[s, 1, c : c + 1, :] = jnp.zeros((1, cells_z), jnp.float32)

    current = [fields[c] for c in range(comps)]
    put_state(0, current)
    pl.semaphore_wait(barrier, wide + narrow - 2)

    copies = halo_copies(0)
    for copy in copies:
        copy.start()
    pending = list(copies)

    total = jnp.zeros((columns, columns), jnp.float32)
    for c in range(comps):
        loads[c].wait()
        last = modes[c, keep:prior, :].astype(jnp.float32)
        last = jnp.concatenate([last, jnp.zeros((columns - prior, mode_lanes), jnp.float32)], 0)
        tail[c] = last.astype(jnp.bfloat16)
        x = jnp.concatenate([modes[c, 0:keep, :], tail[c]], 0)
        total = total + lax.dot_general(x, x, NT, preferred_element_type=jnp.float32)
    gram[...] = total
    mine = pl.ds(pl.multiple_of(iw * piece_rows, piece_rows), piece_rows)
    scatter[iw] = gram[mine, :]
    first = []
    for d in range(1, wide):
        peer = w_peer(d)
        theirs = pl.ds(pl.multiple_of(peer * piece_rows, piece_rows), piece_rows)
        first.append(remote(gram.at[theirs], scatter.at[iw], red_send.at[0, d], red_recv.at[0, iw], (peer, jn)))
    for copy in first:
        copy.start()
    pending += first

    def reduce_step(s):
        started = []
        if s == 1:
            for d in range(1, wide):
                peer = w_peer(d)
                remote(gram.at[mine], scatter.at[peer], red_send.at[0, d], red_recv.at[0, peer], (peer, jn)).wait_recv()
            acc = scatter[0]
            for w in range(1, wide):
                acc = acc + scatter[w]
            part[...] = acc
            share[jn] = acc
            for d in range(1, narrow):
                started.append(remote(part, share.at[jn], red_send.at[1, d], red_recv.at[1, jn], (iw, n_peer(d))))
        elif s == 2:
            for d in range(1, narrow):
                peer = n_peer(d)
                remote(part, share.at[peer], red_send.at[1, d], red_recv.at[1, peer], (iw, peer)).wait_recv()
            acc = share[0]
            for n in range(1, narrow):
                acc = acc + share[n]
            piece[...] = acc
            whole[iw] = acc
            for d in range(1, wide):
                started.append(remote(piece, whole.at[iw], red_send.at[2, d], red_recv.at[2, iw], (w_peer(d), jn)))
        elif s == 3:
            for d in range(1, wide):
                peer = w_peer(d)
                remote(piece, whole.at[peer], red_send.at[2, d], red_recv.at[2, peer], (peer, jn)).wait_recv()
        for copy in started:
            copy.start()
        return started

    def send_snapshot(s, values):
        stacked = jnp.concatenate(values + [jnp.zeros((snap_out.shape[2] - comps * cells_y, cells_z), jnp.float32)], 0)
        stacked = stacked.astype(jnp.bfloat16)
        for b in range(cells_z // LANES):
            snap_out[s, b] = stacked[:, b * LANES : (b + 1) * LANES]
        snap_in[s, jn] = snap_out[s, (jn * z_own) // LANES]
        started = []
        for d in range(1, narrow):
            peer = n_peer(d)
            started.append(
                remote(snap_out.at[s, (peer * z_own) // LANES], snap_in.at[s, jn],
                       snap_send.at[s, d], snap_recv.at[s, jn], (iw, peer))
            )
        for copy in started:
            copy.start()
        return started

    row = lax.broadcasted_iota(jnp.int32, (cells_y, cells_z), 0)
    base = current
    for s in range(stages):
        for copy in copies:
            copy.wait_recv()
        x_low = [x_halo[s, 0, c] for c in range(comps)]
        x_high = [x_halo[s, 1, c] for c in range(comps)]
        y_low, y_high = [], []
        for c in range(comps):
            low = jnp.broadcast_to(y_halo[s, 0, c : c + 1, :], (cells_y, cells_z))
            high = jnp.broadcast_to(y_halo[s, 1, c : c + 1, :], (cells_y, cells_z))
            y_low.append(jnp.where(row == 0, low, pltpu.roll(current[c], 1, 0)))
            y_high.append(jnp.where(row == cells_y - 1, high, pltpu.roll(current[c], cells_y - 1, 0)))
        change = tendency(current, x_low, x_high, y_low, y_high)
        moved = [a + TIME_STEP * b for a, b in zip(current, change)]
        if s % 2 == 1:
            moved = [0.5 * a + 0.5 * b for a, b in zip(base, moved)]
            base = moved
        current = moved
        if s + 1 < stages:
            put_state(s + 1, current)
            copies = halo_copies(s + 1)
            for copy in copies:
                copy.start()
            pending += copies
        pending += send_snapshot(s, current)
        pending += reduce_step(s + 1)
    for c in range(comps):
        flow[c] = current[c]

    offset = lax.rem(jn * z_own, LANES)
    spread = (
        lax.rem(lax.broadcasted_iota(jnp.int32, (LANES, y_all), 0), y_all)
        == lax.broadcasted_iota(jnp.int32, (LANES, y_all), 1)
    ).astype(jnp.bfloat16)
    z_id = lax.broadcasted_iota(jnp.int32, (LANES, LANES), 1) - offset
    k_id = lax.broadcasted_iota(jnp.int32, (LANES, LANES), 0) // y_all
    fits = lax.rem(z_id + LANES, z_group) == k_id
    pick_row = lax.broadcasted_iota(jnp.int32, (16 * groups, LANES), 0)
    pick_z = lax.broadcasted_iota(jnp.int32, (16 * groups, LANES), 1) - offset
    inside = (pick_z >= 0) & (pick_z // z_group == pick_row // 16)
    acc = [jnp.zeros((16 * groups, LANES), jnp.float32) for _ in range(comps)]
    for s in range(stages):
        for d in range(1, narrow):
            peer = n_peer(d)
            remote(snap_out.at[s, 0], snap_in.at[s, peer], snap_send.at[s, d], snap_recv.at[s, peer], (iw, peer)).wait_recv()
        arrived = [snap_in[s, n].astype(jnp.float32) for n in range(narrow)]
        pick = (inside & (lax.rem(pick_row, 16) == 16 - stages + s)).astype(jnp.bfloat16)
        for c in range(comps):
            cells = jnp.concatenate([a[c * cells_y : (c + 1) * cells_y, :] for a in arrived], 0)
            wide_cells = jnp.dot(spread, cells.astype(jnp.bfloat16), preferred_element_type=jnp.float32)
            chosen = jnp.where(fits, wide_cells, 0.0).astype(jnp.bfloat16)
            acc[c] = acc[c] + lax.dot_general(pick, chosen, NT, preferred_element_type=jnp.float32)
    total = jnp.zeros((16, columns), jnp.float32)
    for c in range(comps):
        flat = jnp.concatenate([acc[c][16 * g : 16 * g + 16, :] for g in range(groups)], 1)
        rows = (tail[c].astype(jnp.float32) + flat).astype(jnp.bfloat16)
        x = jnp.concatenate([modes[c, 0:keep, :], rows], 0)
        total = total + lax.dot_general(rows, x, NT, preferred_element_type=jnp.float32)
    mine8 = total[8:16, :]
    rows8[...] = mine8
    rows_n[jn] = mine8
    started = [
        remote(rows8, rows_n.at[jn], last_send.at[0, d], last_recv.at[0, jn], (iw, n_peer(d)))
        for d in range(1, narrow)
    ]
    for copy in started:
        copy.start()
    pending += started
    for d in range(1, narrow):
        peer = n_peer(d)
        remote(rows8, rows_n.at[peer], last_send.at[0, d], last_recv.at[0, peer], (iw, peer)).wait_recv()
    sum8 = rows_n[0]
    for n in range(1, narrow):
        sum8 = sum8 + rows_n[n]
    sums8[...] = sum8
    rows_w[iw] = sum8
    started = [
        remote(sums8, rows_w.at[iw], last_send.at[1, d], last_recv.at[1, iw], (w_peer(d), jn))
        for d in range(1, wide)
    ]
    for copy in started:
        copy.start()
    pending += started
    for d in range(1, wide):
        peer = w_peer(d)
        remote(sums8, rows_w.at[peer], last_send.at[1, d], last_recv.at[1, peer], (peer, jn)).wait_recv()
    sum8 = rows_w[0]
    for w in range(1, wide):
        sum8 = sum8 + rows_w[w]
    for copy in pending:
        copy.wait_send()

    inverse_cells = 1.0 / (wide * narrow * cells_y * cells_z)
    old = jnp.concatenate([whole[w] for w in range(wide)], 0)
    bottom = jnp.concatenate([jnp.zeros((columns - 8, columns), jnp.float32), sum8], 0)
    side = jnp.transpose(bottom)
    row = lax.broadcasted_iota(jnp.int32, (columns, columns), 0)
    col = lax.broadcasted_iota(jnp.int32, (columns, columns), 1)
    full = jnp.where(row >= prior, bottom, jnp.where(col >= prior, side, old))
    gram_out[...] = full * inverse_cells


def local(wide, narrow, fields, prior_modes):
    comps, cells_x, cells_y, cells_z = fields.shape
    prior = prior_modes.shape[0]
    stages = 2 * STEPS
    columns = prior + stages
    modes = jnp.transpose(prior_modes, (1, 2, 0, 3)).reshape(comps, prior, prior_modes.shape[3])
    piece = columns // wide
    snap_rows = -(-comps * cells_y // 16) * 16
    f32, bf16 = jnp.float32, jnp.bfloat16
    vmem = pl.BlockSpec(memory_space=pltpu.VMEM)
    dma = pltpu.SemaphoreType.DMA
    flow, gram = pl.pallas_call(
        functools.partial(kernel, wide, narrow),
        out_shape=(
            jax.ShapeDtypeStruct((comps, cells_y, cells_z), f32),
            jax.ShapeDtypeStruct((columns, columns), f32),
        ),
        in_specs=[vmem, pl.BlockSpec(memory_space=pl.ANY)],
        out_specs=(vmem, vmem),
        scratch_shapes=[
            pltpu.VMEM(modes.shape, bf16), dma((comps,)),
            pltpu.VMEM((stages, comps, cells_y, cells_z), f32),
            pltpu.VMEM((stages, 2, comps, cells_y, cells_z), f32),
            pltpu.VMEM((stages, 2, 8, cells_z), f32),
            pltpu.VMEM((stages, 2, 8, cells_z), f32),
            dma((stages, 4)), dma((stages, 4)),
            pltpu.VMEM((stages, cells_z // LANES, snap_rows, LANES), bf16),
            pltpu.VMEM((stages, narrow, snap_rows, LANES), bf16),
            dma((stages, narrow)), dma((stages, narrow)),
            pltpu.VMEM((columns, columns), f32),
            pltpu.VMEM((wide, piece, columns), f32),
            pltpu.VMEM((piece, columns), f32),
            pltpu.VMEM((narrow, piece, columns), f32),
            pltpu.VMEM((wide, piece, columns), f32),
            pltpu.VMEM((piece, columns), f32),
            dma((3, max(wide, narrow))), dma((3, max(wide, narrow))),
            pltpu.VMEM((comps, 16, modes.shape[2]), bf16),
            pltpu.VMEM((8, columns), f32),
            pltpu.VMEM((narrow, 8, columns), f32),
            pltpu.VMEM((8, columns), f32),
            pltpu.VMEM((wide, 8, columns), f32),
            dma((2, max(wide, narrow))), dma((2, max(wide, narrow))),
        ],
        compiler_params=pltpu.CompilerParams(
            collective_id=0, has_side_effects=True, vmem_limit_bytes=24 * 1024 * 1024
        ),
    )(fields.reshape(comps, cells_y, cells_z), modes)
    factor = pl.pallas_call(
        factor_kernel,
        out_shape=jax.ShapeDtypeStruct((columns, columns), f32),
        in_specs=[vmem],
        out_specs=vmem,
    )(gram)
    return flow.reshape(fields.shape), factor


def solution(mesh):
    wide, narrow = mesh.shape["wide"], mesh.shape["narrow"]
    return jax.shard_map(
        functools.partial(local, wide, narrow),
        mesh=mesh,
        in_specs=(P(None, "wide", "narrow", None), P(None, None, "wide", "narrow")),
        out_specs=(P(None, "wide", "narrow", None), P()),
        check_vma=False,
    )
```

```python
import functools

import jax
import jax.numpy as jnp
from jax import lax
from jax.experimental import pallas as pl
from jax.experimental.pallas import tpu as pltpu
from jax.sharding import PartitionSpec as P

STEPS = 2
GAMMA = 1.4
TIME_STEP = 0.25
VISCOSITY = 0.15
LANES = 128
NT = (((1,), (1,)), ((), ()))


def flux_of(state, d):
    density, energy = state[0], state[4]
    momentum = state[1:4]
    inverse = 1.0 / density
    vel = momentum[d] * inverse
    squares = momentum[0] * momentum[0] + momentum[1] * momentum[1] + momentum[2] * momentum[2]
    pressure = (GAMMA - 1.0) * (energy - 0.5 * squares * inverse)
    out = [momentum[d], momentum[0] * vel, momentum[1] * vel, momentum[2] * vel]
    out.append((energy + pressure) * vel)
    out[1 + d] = out[1 + d] + pressure
    return out


def tendency(here, x_low, x_high, y_low, y_high):
    cells_z = here[0].shape[1]
    z_low = [pltpu.roll(c, 1, 1) for c in here]
    z_high = [pltpu.roll(c, cells_z - 1, 1) for c in here]
    total = None
    for d, (low, high) in enumerate(((x_low, x_high), (y_low, y_high), (z_low, z_high))):
        flux_low, flux_high = flux_of(low, d), flux_of(high, d)
        part = [
            -0.5 * (fh - fl) + VISCOSITY * (l + h)
            for fh, fl, l, h in zip(flux_high, flux_low, low, high)
        ]
        total = part if total is None else [a + b for a, b in zip(total, part)]
    return [t - (6.0 * VISCOSITY) * c for t, c in zip(total, here)]


def lane_ids():
    return lax.broadcasted_iota(jnp.int32, (8, LANES), 1)


def row_ids():
    return lax.broadcasted_iota(jnp.int32, (8, LANES), 0)


def column_of(tile, j):
    return jnp.broadcast_to(tile[:, j : j + 1], (8, LANES))


def row_of(tile, k):
    return jnp.broadcast_to(tile[k : k + 1, :], (8, LANES))


def inverted(x):
    guess = pl.reciprocal(x, approx=True)
    guess = guess * (2.0 - x * guess)
    return guess * (2.0 - x * guess)


def eliminate_panel(tiles, p, first, last):
    lane, row = lane_ids(), row_ids()
    pivots = jnp.zeros((8, LANES), jnp.float32)
    steps = range(first, last)
    panel = tiles[p]
    columns = {k: column_of(panel, 8 * p + k) for k in steps}
    heads, inverses, crossings = {}, {}, {}
    for k in steps:
        j = 8 * p + k
        pivot = row_of(columns[k], k)
        inverses[k] = inverted(pivot)
        pivots = jnp.where(row == k, pivot, pivots)
        factor = jnp.where(row > k, columns[k], 0.0) * inverses[k]
        for m in steps:
            if m > k:
                crossings[k, m] = row_of(columns[m], k)
                columns[m] = columns[m] - factor * crossings[k, m]
        heads[k] = jnp.where(lane == j, 1.0, row_of(panel, k))
        panel = jnp.where((lane == j) & (row > k), 0.0, panel) - factor * heads[k]
    tiles[p] = panel
    cleared = (lane >= 8 * p + first) & (lane < 8 * p + last)
    for t in range(p + 1, len(tiles)):
        columns = {k: column_of(tiles[t], 8 * p + k) for k in steps}
        rest = jnp.where(cleared, 0.0, tiles[t])
        for k in steps:
            factor = columns[k] * inverses[k]
            for m in steps:
                if m > k:
                    columns[m] = columns[m] - factor * crossings[k, m]
            outside = jnp.where((lane > 8 * p + k) & cleared, 0.0, heads[k])
            rest = rest - factor * outside
        tiles[t] = rest
    return pivots


def kernel(
    wide, narrow, fields, modes_hbm, flow, factor_out,
    modes, modes_sem, fields_sem, state, x_halo, y_send, y_halo, halo_send, halo_recv,
    snap_out, snap_in, snap_send, snap_recv,
    gram, scatter, part, share, whole, piece, red_send, red_recv,
    tail, rows8, rows_n, sums8, rows_w, last_send, last_recv,
):
    stages = 2 * STEPS
    comps, cells_y, cells_z = fields.shape
    prior = modes.shape[1]
    columns = gram.shape[0]
    mode_lanes = modes.shape[2]
    y_all = cells_y * narrow
    z_own = cells_z // narrow
    z_group = LANES // y_all
    groups = mode_lanes // LANES
    piece_rows = columns // wide
    keep = columns - 16
    iw, jn = lax.axis_index("wide"), lax.axis_index("narrow")

    def w_peer(d):
        return lax.rem(iw + d, wide)

    def n_peer(d):
        return lax.rem(jn + d, narrow)

    def remote(src, dst, send, recv, device):
        return pltpu.make_async_remote_copy(
            src_ref=src, dst_ref=dst, send_sem=send, recv_sem=recv,
            device_id=device, device_id_type=pl.DeviceIdType.MESH,
        )

    loads = [pltpu.make_async_copy(modes_hbm.at[c], modes.at[c], modes_sem.at[c]) for c in range(comps)]
    fields_load = pltpu.make_async_copy(fields, state.at[0], fields_sem.at[0])
    fields_load.start()
    for load in loads:
        load.start()

    barrier = pltpu.get_barrier_semaphore()
    for d in range(1, wide):
        pl.semaphore_signal(barrier, inc=1, device_id=(w_peer(d), jn), device_id_type=pl.DeviceIdType.MESH)
    for d in range(1, narrow):
        pl.semaphore_signal(barrier, inc=1, device_id=(iw, n_peer(d)), device_id_type=pl.DeviceIdType.MESH)

    def halo_copies(s):
        right, left = (w_peer(1), jn), (w_peer(wide - 1), jn)
        up, down = (iw, n_peer(1)), (iw, n_peer(narrow - 1))
        return [
            remote(state.at[s], x_halo.at[s, 0], halo_send.at[s, 0], halo_recv.at[s, 0], right),
            remote(state.at[s], x_halo.at[s, 1], halo_send.at[s, 1], halo_recv.at[s, 1], left),
            remote(y_send.at[s, 1], y_halo.at[s, 0], halo_send.at[s, 2], halo_recv.at[s, 2], up),
            remote(y_send.at[s, 0], y_halo.at[s, 1], halo_send.at[s, 3], halo_recv.at[s, 3], down),
        ]

    def put_state(s, values):
        for c in range(comps):
            if s > 0:
                state[s, c] = values[c]
            y_send[s, 0, c : c + 1, :] = values[c][0:1, :]
            y_send[s, 1, c : c + 1, :] = values[c][cells_y - 1 : cells_y, :]
        for c in range(comps, 8):
            y_send[s, 0, c : c + 1, :] = jnp.zeros((1, cells_z), jnp.float32)
            y_send[s, 1, c : c + 1, :] = jnp.zeros((1, cells_z), jnp.float32)

    fields_load.wait()
    current = [state[0, c] for c in range(comps)]
    put_state(0, current)
    pl.semaphore_wait(barrier, wide + narrow - 2)

    copies = halo_copies(0)
    for copy in copies:
        copy.start()
    pending = list(copies)

    total = jnp.zeros((columns, columns), jnp.float32)
    for c in range(comps):
        loads[c].wait()
        last = modes[c, keep:prior, :].astype(jnp.float32)
        last = jnp.concatenate([last, jnp.zeros((columns - prior, mode_lanes), jnp.float32)], 0)
        tail[c] = last.astype(jnp.bfloat16)
        x = jnp.concatenate([modes[c, 0:keep, :], tail[c]], 0)
        total = total + lax.dot_general(x, x, NT, preferred_element_type=jnp.float32)
    gram[...] = total
    mine = pl.ds(pl.multiple_of(iw * piece_rows, piece_rows), piece_rows)
    scatter[iw] = gram[mine, :]
    first = []
    for d in range(1, wide):
        peer = w_peer(d)
        theirs = pl.ds(pl.multiple_of(peer * piece_rows, piece_rows), piece_rows)
        first.append(remote(gram.at[theirs], scatter.at[iw], red_send.at[0, d], red_recv.at[0, iw], (peer, jn)))
    for copy in first:
        copy.start()
    pending += first

    def reduce_step(s):
        started = []
        if s == 1:
            for d in range(1, wide):
                peer = w_peer(d)
                remote(gram.at[mine], scatter.at[peer], red_send.at[0, d], red_recv.at[0, peer], (peer, jn)).wait_recv()
            acc = scatter[0]
            for w in range(1, wide):
                acc = acc + scatter[w]
            part[...] = acc
            share[jn] = acc
            for d in range(1, narrow):
                started.append(remote(part, share.at[jn], red_send.at[1, d], red_recv.at[1, jn], (iw, n_peer(d))))
        elif s == 2:
            for d in range(1, narrow):
                peer = n_peer(d)
                remote(part, share.at[peer], red_send.at[1, d], red_recv.at[1, peer], (iw, peer)).wait_recv()
            acc = share[0]
            for n in range(1, narrow):
                acc = acc + share[n]
            piece[...] = acc
            whole[iw] = acc
            for d in range(1, wide):
                started.append(remote(piece, whole.at[iw], red_send.at[2, d], red_recv.at[2, iw], (w_peer(d), jn)))
        elif s == 3:
            for d in range(1, wide):
                peer = w_peer(d)
                remote(piece, whole.at[peer], red_send.at[2, d], red_recv.at[2, peer], (peer, jn)).wait_recv()
        for copy in started:
            copy.start()
        return started

    def send_snapshot(s, values):
        stacked = jnp.concatenate(values + [jnp.zeros((snap_out.shape[2] - comps * cells_y, cells_z), jnp.float32)], 0)
        stacked = stacked.astype(jnp.bfloat16)
        for b in range(cells_z // LANES):
            snap_out[s, b] = stacked[:, b * LANES : (b + 1) * LANES]
        snap_in[s, jn] = snap_out[s, (jn * z_own) // LANES]
        started = []
        for d in range(1, narrow):
            peer = n_peer(d)
            started.append(
                remote(snap_out.at[s, (peer * z_own) // LANES], snap_in.at[s, jn],
                       snap_send.at[s, d], snap_recv.at[s, jn], (iw, peer))
            )
        for copy in started:
            copy.start()
        return started

    offset = lax.rem(jn * z_own, LANES)
    spread = (
        lax.rem(lax.broadcasted_iota(jnp.int32, (LANES, y_all), 0), y_all)
        == lax.broadcasted_iota(jnp.int32, (LANES, y_all), 1)
    ).astype(jnp.bfloat16)
    z_id = lax.broadcasted_iota(jnp.int32, (LANES, LANES), 1) - offset
    k_id = lax.broadcasted_iota(jnp.int32, (LANES, LANES), 0) // y_all
    fits = lax.rem(z_id + LANES, z_group) == k_id
    pick_row = lax.broadcasted_iota(jnp.int32, (16 * groups, LANES), 0)
    pick_z = lax.broadcasted_iota(jnp.int32, (16 * groups, LANES), 1) - offset
    inside = (pick_z >= 0) & (pick_z // z_group == pick_row // 16)
    acc = [jnp.zeros((16 * groups, LANES), jnp.float32) for _ in range(comps)]

    def order_snapshot(s):
        for d in range(1, narrow):
            peer = n_peer(d)
            remote(snap_out.at[s, 0], snap_in.at[s, peer], snap_send.at[s, d], snap_recv.at[s, peer], (iw, peer)).wait_recv()
        arrived = [snap_in[s, n].astype(jnp.float32) for n in range(narrow)]
        pick = (inside & (lax.rem(pick_row, 16) == 16 - stages + s)).astype(jnp.bfloat16)
        for c in range(comps):
            cells = jnp.concatenate([a[c * cells_y : (c + 1) * cells_y, :] for a in arrived], 0)
            wide_cells = jnp.dot(spread, cells.astype(jnp.bfloat16), preferred_element_type=jnp.float32)
            chosen = jnp.where(fits, wide_cells, 0.0).astype(jnp.bfloat16)
            acc[c] = acc[c] + lax.dot_general(pick, chosen, NT, preferred_element_type=jnp.float32)

    tiles, pivots = [], []
    inverse_cells = 1.0 / (wide * narrow * cells_y * cells_z)

    def begin():
        for t in range(columns // 8):
            rows = whole[(8 * t) // piece_rows, (8 * t) % piece_rows : (8 * t) % piece_rows + 8, :]
            tiles.append(rows * inverse_cells)

    def run(start, stop):
        for p in range(start, stop):
            pivots.append(eliminate_panel(tiles, p, 0, min(8, prior - 8 * p)))

    row = lax.broadcasted_iota(jnp.int32, (cells_y, cells_z), 0)
    base = current
    for s in range(stages):
        for copy in copies:
            copy.wait_recv()
        x_low = [x_halo[s, 0, c] for c in range(comps)]
        x_high = [x_halo[s, 1, c] for c in range(comps)]
        y_low, y_high = [], []
        for c in range(comps):
            low = jnp.broadcast_to(y_halo[s, 0, c : c + 1, :], (cells_y, cells_z))
            high = jnp.broadcast_to(y_halo[s, 1, c : c + 1, :], (cells_y, cells_z))
            y_low.append(jnp.where(row == 0, low, pltpu.roll(current[c], 1, 0)))
            y_high.append(jnp.where(row == cells_y - 1, high, pltpu.roll(current[c], cells_y - 1, 0)))
        change = tendency(current, x_low, x_high, y_low, y_high)
        moved = [a + TIME_STEP * b for a, b in zip(current, change)]
        if s % 2 == 1:
            moved = [0.5 * a + 0.5 * b for a, b in zip(base, moved)]
            base = moved
        current = moved
        if s + 1 < stages:
            put_state(s + 1, current)
            copies = halo_copies(s + 1)
            for copy in copies:
                copy.start()
            pending += copies
        pending += send_snapshot(s, current)
        pending += reduce_step(s + 1)
        if s > 0:
            order_snapshot(s - 1)
        if s == stages - 2:
            begin()
            run(0, 4)
    for c in range(comps):
        flow[c] = current[c]

    run(4, 8)
    order_snapshot(stages - 1)
    total = jnp.zeros((16, columns), jnp.float32)
    for c in range(comps):
        flat = jnp.concatenate([acc[c][16 * g : 16 * g + 16, :] for g in range(groups)], 1)
        rows = (tail[c].astype(jnp.float32) + flat).astype(jnp.bfloat16)
        x = jnp.concatenate([modes[c, 0:keep, :], rows], 0)
        total = total + lax.dot_general(rows, x, NT, preferred_element_type=jnp.float32)
    mine8 = total[8:16, :]
    rows8[...] = mine8
    rows_n[jn] = mine8
    started = [
        remote(rows8, rows_n.at[jn], last_send.at[0, d], last_recv.at[0, jn], (iw, n_peer(d)))
        for d in range(1, narrow)
    ]
    for copy in started:
        copy.start()
    pending += started
    run(8, 12)
    for d in range(1, narrow):
        peer = n_peer(d)
        remote(rows8, rows_n.at[peer], last_send.at[0, d], last_recv.at[0, peer], (iw, peer)).wait_recv()
    sum8 = rows_n[0]
    for n in range(1, narrow):
        sum8 = sum8 + rows_n[n]
    sums8[...] = sum8
    rows_w[iw] = sum8
    started = [
        remote(sums8, rows_w.at[iw], last_send.at[1, d], last_recv.at[1, iw], (w_peer(d), jn))
        for d in range(1, wide)
    ]
    for copy in started:
        copy.start()
    pending += started
    run(12, columns // 8)
    lane, row = lane_ids(), row_ids()
    uppers, inverse = [], []
    for t in range(columns // 8):
        scale = lax.rsqrt(jnp.where(pivots[t] > 0.0, pivots[t], 1.0))
        scale = jnp.where(row + 8 * t < prior, scale, 0.0)
        uppers.append(jnp.where(lane >= row + 8 * t, tiles[t], 0.0) * scale)
        left = jnp.where(lane < row + 8 * t, tiles[t], 0.0)
        inverse.append(jnp.where(lane == row + 8 * t, 1.0, left) * scale)
    inverse = jnp.concatenate(inverse, 0)
    for copy in pending:
        copy.wait_send()
    for d in range(1, wide):
        peer = w_peer(d)
        remote(sums8, rows_w.at[peer], last_send.at[1, d], last_recv.at[1, peer], (peer, jn)).wait_recv()
    sum8 = rows_w[0]
    for w in range(1, wide):
        sum8 = sum8 + rows_w[w]

    exact = lax.Precision.HIGHEST
    corner = row + columns - 8 >= prior
    rows = jnp.where(corner, sum8 * inverse_cells, 0.0)
    known = jnp.where(lane < prior, rows, 0.0)
    solved = lax.dot_general(known, inverse, NT, precision=exact, preferred_element_type=jnp.float32)
    bottom = jnp.concatenate([jnp.zeros((columns - 8, columns), jnp.float32), solved], 0)
    taken = lax.dot_general(solved, bottom, NT, precision=exact, preferred_element_type=jnp.float32)
    last_tile = [jnp.where(lane >= prior, rows - taken, 0.0)]
    last_tile = [pltpu.roll(last_tile[0], 8, 1)]
    left = eliminate_panel(last_tile, 0, prior - (columns - 8), 8)
    tip = jnp.where(lane >= row, last_tile[0], 0.0) * lax.rsqrt(jnp.where(corner, left, 1.0))
    tip = pltpu.roll(jnp.where(corner, tip, 0.0), LANES - 8, 1)
    side = jnp.transpose(bottom)
    for t in range(columns // 8):
        out = uppers[t] + side[8 * t : 8 * t + 8, :]
        if t == columns // 8 - 1:
            out = jnp.where(corner, tip, out)
        factor_out[8 * t : 8 * t + 8, :] = out


def local(wide, narrow, fields, prior_modes):
    comps, cells_x, cells_y, cells_z = fields.shape
    prior = prior_modes.shape[0]
    stages = 2 * STEPS
    columns = prior + stages
    modes = jnp.transpose(prior_modes, (1, 2, 0, 3)).reshape(comps, prior, prior_modes.shape[3])
    piece = columns // wide
    snap_rows = -(-comps * cells_y // 16) * 16
    f32, bf16 = jnp.float32, jnp.bfloat16
    vmem = pl.BlockSpec(memory_space=pltpu.VMEM)
    dma = pltpu.SemaphoreType.DMA
    flow, factor = pl.pallas_call(
        functools.partial(kernel, wide, narrow),
        out_shape=(
            jax.ShapeDtypeStruct((comps, cells_y, cells_z), f32),
            jax.ShapeDtypeStruct((columns, columns), f32),
        ),
        in_specs=[pl.BlockSpec(memory_space=pl.ANY)] * 2,
        out_specs=(vmem, vmem),
        scratch_shapes=[
            pltpu.VMEM(modes.shape, bf16), dma((comps,)), dma((1,)),
            pltpu.VMEM((stages, comps, cells_y, cells_z), f32),
            pltpu.VMEM((stages, 2, comps, cells_y, cells_z), f32),
            pltpu.VMEM((stages, 2, 8, cells_z), f32),
            pltpu.VMEM((stages, 2, 8, cells_z), f32),
            dma((stages, 4)), dma((stages, 4)),
            pltpu.VMEM((stages, cells_z // LANES, snap_rows, LANES), bf16),
            pltpu.VMEM((stages, narrow, snap_rows, LANES), bf16),
            dma((stages, narrow)), dma((stages, narrow)),
            pltpu.VMEM((columns, columns), f32),
            pltpu.VMEM((wide, piece, columns), f32),
            pltpu.VMEM((piece, columns), f32),
            pltpu.VMEM((narrow, piece, columns), f32),
            pltpu.VMEM((wide, piece, columns), f32),
            pltpu.VMEM((piece, columns), f32),
            dma((3, max(wide, narrow))), dma((3, max(wide, narrow))),
            pltpu.VMEM((comps, 16, modes.shape[2]), bf16),
            pltpu.VMEM((8, columns), f32),
            pltpu.VMEM((narrow, 8, columns), f32),
            pltpu.VMEM((8, columns), f32),
            pltpu.VMEM((wide, 8, columns), f32),
            dma((2, max(wide, narrow))), dma((2, max(wide, narrow))),
        ],
        compiler_params=pltpu.CompilerParams(
            collective_id=0, has_side_effects=True, vmem_limit_bytes=60 * 1024 * 1024
        ),
    )(fields.reshape(comps, cells_y, cells_z), modes)
    return flow.reshape(fields.shape), factor


def solution(mesh):
    wide, narrow = mesh.shape["wide"], mesh.shape["narrow"]
    return jax.shard_map(
        functools.partial(local, wide, narrow),
        mesh=mesh,
        in_specs=(P(None, "wide", "narrow", None), P(None, None, "wide", "narrow")),
        out_specs=(P(None, "wide", "narrow", None), P()),
        check_vma=False,
    )
```

```python
import functools

import jax
import jax.numpy as jnp
from jax import lax
from jax.experimental import pallas as pl
from jax.experimental.pallas import tpu as pltpu
from jax.sharding import PartitionSpec as P

STEPS = 2
GAMMA = 1.4
TIME_STEP = 0.25
VISCOSITY = 0.15
LANES = 128
NT = (((1,), (1,)), ((), ()))


def flux_of(state, d):
    density, energy = state[0], state[4]
    momentum = state[1:4]
    inverse = 1.0 / density
    vel = momentum[d] * inverse
    squares = momentum[0] * momentum[0] + momentum[1] * momentum[1] + momentum[2] * momentum[2]
    pressure = (GAMMA - 1.0) * (energy - 0.5 * squares * inverse)
    out = [momentum[d], momentum[0] * vel, momentum[1] * vel, momentum[2] * vel]
    out.append((energy + pressure) * vel)
    out[1 + d] = out[1 + d] + pressure
    return out


def tendency(here, x_low, x_high, y_low, y_high):
    cells_z = here[0].shape[1]
    z_low = [pltpu.roll(c, 1, 1) for c in here]
    z_high = [pltpu.roll(c, cells_z - 1, 1) for c in here]
    total = None
    for d, (low, high) in enumerate(((x_low, x_high), (y_low, y_high), (z_low, z_high))):
        flux_low, flux_high = flux_of(low, d), flux_of(high, d)
        part = [
            -0.5 * (fh - fl) + VISCOSITY * (l + h)
            for fh, fl, l, h in zip(flux_high, flux_low, low, high)
        ]
        total = part if total is None else [a + b for a, b in zip(total, part)]
    return [t - (6.0 * VISCOSITY) * c for t, c in zip(total, here)]


def lane_ids():
    return lax.broadcasted_iota(jnp.int32, (8, LANES), 1)


def row_ids():
    return lax.broadcasted_iota(jnp.int32, (8, LANES), 0)


def column_of(tile, j):
    return jnp.broadcast_to(tile[:, j : j + 1], (8, LANES))


def row_of(tile, k):
    return jnp.broadcast_to(tile[k : k + 1, :], (8, LANES))


def inverted(x):
    guess = pl.reciprocal(x, approx=True)
    guess = guess * (2.0 - x * guess)
    return guess * (2.0 - x * guess)


def eliminate_panel(tiles, p, first, last):
    lane, row = lane_ids(), row_ids()
    pivots = jnp.zeros((8, LANES), jnp.float32)
    steps = range(first, last)
    panel = tiles[p]
    columns = {k: column_of(panel, 8 * p + k) for k in steps}
    heads, inverses, crossings = {}, {}, {}
    for k in steps:
        j = 8 * p + k
        pivot = row_of(columns[k], k)
        inverses[k] = inverted(pivot)
        pivots = jnp.where(row == k, pivot, pivots)
        factor = jnp.where(row > k, columns[k], 0.0) * inverses[k]
        for m in steps:
            if m > k:
                crossings[k, m] = row_of(columns[m], k)
                columns[m] = columns[m] - factor * crossings[k, m]
        heads[k] = jnp.where(lane == j, 1.0, row_of(panel, k))
        panel = jnp.where((lane == j) & (row > k), 0.0, panel) - factor * heads[k]
    tiles[p] = panel
    cleared = (lane >= 8 * p + first) & (lane < 8 * p + last)
    for t in range(p + 1, len(tiles)):
        columns = {k: column_of(tiles[t], 8 * p + k) for k in steps}
        rest = jnp.where(cleared, 0.0, tiles[t])
        for k in steps:
            factor = columns[k] * inverses[k]
            for m in steps:
                if m > k:
                    columns[m] = columns[m] - factor * crossings[k, m]
            outside = jnp.where((lane > 8 * p + k) & cleared, 0.0, heads[k])
            rest = rest - factor * outside
        tiles[t] = rest
    return pivots


def kernel(
    wide, narrow, fields, modes_hbm, flow, factor_out,
    modes, modes_sem, start, start_sem, packed, x_halo, y_send, y_halo, halo_send, halo_recv,
    snap_in, snap_send, snap_recv,
    gram, scatter, part, share, whole, piece, red_send, red_recv,
    tail, rows8, rows_n, sums8, rows_w, last_send, last_recv,
):
    stages = 2 * STEPS
    comps, cells_y, cells_z = fields.shape
    prior = modes.shape[1]
    columns = gram.shape[0]
    mode_lanes = modes.shape[2]
    y_all = cells_y * narrow
    z_own = cells_z // narrow
    z_group = LANES // y_all
    groups = mode_lanes // LANES
    piece_rows = columns // wide
    keep = columns - 16
    iw, jn = lax.axis_index("wide"), lax.axis_index("narrow")

    def w_peer(d):
        return lax.rem(iw + d, wide)

    def n_peer(d):
        return lax.rem(jn + d, narrow)

    def remote(src, dst, send, recv, device):
        return pltpu.make_async_remote_copy(
            src_ref=src, dst_ref=dst, send_sem=send, recv_sem=recv,
            device_id=device, device_id_type=pl.DeviceIdType.MESH,
        )

    loads = [pltpu.make_async_copy(modes_hbm.at[c], modes.at[c], modes_sem.at[c]) for c in range(comps)]
    fields_load = pltpu.make_async_copy(fields, start, start_sem.at[0])
    fields_load.start()
    for load in loads:
        load.start()

    barrier = pltpu.get_barrier_semaphore()
    for d in range(1, wide):
        pl.semaphore_signal(barrier, inc=1, device_id=(w_peer(d), jn), device_id_type=pl.DeviceIdType.MESH)
    for d in range(1, narrow):
        pl.semaphore_signal(barrier, inc=1, device_id=(iw, n_peer(d)), device_id_type=pl.DeviceIdType.MESH)

    def halo_copies(s):
        right, left = (w_peer(1), jn), (w_peer(wide - 1), jn)
        up, down = (iw, n_peer(1)), (iw, n_peer(narrow - 1))
        return [
            remote(packed.at[s], x_halo.at[s, 0], halo_send.at[s, 0], halo_recv.at[s, 0], right),
            remote(packed.at[s], x_halo.at[s, 1], halo_send.at[s, 1], halo_recv.at[s, 1], left),
            remote(y_send.at[s, 1], y_halo.at[s, 0], halo_send.at[s, 2], halo_recv.at[s, 2], up),
            remote(y_send.at[s, 0], y_halo.at[s, 1], halo_send.at[s, 3], halo_recv.at[s, 3], down),
        ]

    def put_state(s, values):
        spare = jnp.zeros((packed.shape[2] - comps * cells_y, cells_z), jnp.float32)
        stacked = jnp.concatenate(values + [spare], 0).astype(jnp.bfloat16)
        for b in range(cells_z // LANES):
            packed[s, b] = stacked[:, b * LANES : (b + 1) * LANES]
        if s < stages:
            for c in range(comps):
                y_send[s, 0, c : c + 1, :] = values[c][0:1, :]
                y_send[s, 1, c : c + 1, :] = values[c][cells_y - 1 : cells_y, :]
            for c in range(comps, 8):
                y_send[s, 0, c : c + 1, :] = jnp.zeros((1, cells_z), jnp.float32)
                y_send[s, 1, c : c + 1, :] = jnp.zeros((1, cells_z), jnp.float32)

    def unpack(ref):
        blocks = [ref[b].astype(jnp.float32) for b in range(cells_z // LANES)]
        return [
            jnp.concatenate([x[c * cells_y : (c + 1) * cells_y, :] for x in blocks], 1)
            for c in range(comps)
        ]

    fields_load.wait()
    current = [start[c] for c in range(comps)]
    put_state(0, current)
    pl.semaphore_wait(barrier, wide + narrow - 2)

    copies = halo_copies(0)
    for copy in copies:
        copy.start()
    pending = list(copies)

    total = jnp.zeros((columns, columns), jnp.float32)
    for c in range(comps):
        loads[c].wait()
        last = modes[c, keep:prior, :].astype(jnp.float32)
        last = jnp.concatenate([last, jnp.zeros((columns - prior, mode_lanes), jnp.float32)], 0)
        tail[c] = last.astype(jnp.bfloat16)
        x = jnp.concatenate([modes[c, 0:keep, :], tail[c]], 0)
        total = total + lax.dot_general(x, x, NT, preferred_element_type=jnp.float32)
    gram[...] = total
    mine = pl.ds(pl.multiple_of(iw * piece_rows, piece_rows), piece_rows)
    scatter[iw] = gram[mine, :]
    first = []
    for d in range(1, wide):
        peer = w_peer(d)
        theirs = pl.ds(pl.multiple_of(peer * piece_rows, piece_rows), piece_rows)
        first.append(remote(gram.at[theirs], scatter.at[iw], red_send.at[0, d], red_recv.at[0, iw], (peer, jn)))
    for copy in first:
        copy.start()
    pending += first

    def reduce_step(s):
        started = []
        if s == 1:
            for d in range(1, wide):
                peer = w_peer(d)
                remote(gram.at[mine], scatter.at[peer], red_send.at[0, d], red_recv.at[0, peer], (peer, jn)).wait_recv()
            acc = scatter[0]
            for w in range(1, wide):
                acc = acc + scatter[w]
            part[...] = acc
            share[jn] = acc
            for d in range(1, narrow):
                started.append(remote(part, share.at[jn], red_send.at[1, d], red_recv.at[1, jn], (iw, n_peer(d))))
        elif s == 2:
            for d in range(1, narrow):
                peer = n_peer(d)
                remote(part, share.at[peer], red_send.at[1, d], red_recv.at[1, peer], (iw, peer)).wait_recv()
            acc = share[0]
            for n in range(1, narrow):
                acc = acc + share[n]
            piece[...] = acc
            whole[iw] = acc
            for d in range(1, wide):
                started.append(remote(piece, whole.at[iw], red_send.at[2, d], red_recv.at[2, iw], (w_peer(d), jn)))
        elif s == 3:
            for d in range(1, wide):
                peer = w_peer(d)
                remote(piece, whole.at[peer], red_send.at[2, d], red_recv.at[2, peer], (peer, jn)).wait_recv()
        for copy in started:
            copy.start()
        return started

    def send_snapshot(s):
        snap_in[s, jn] = packed[s + 1, (jn * z_own) // LANES]
        started = []
        for d in range(1, narrow):
            peer = n_peer(d)
            started.append(
                remote(packed.at[s + 1, (peer * z_own) // LANES], snap_in.at[s, jn],
                       snap_send.at[s, d], snap_recv.at[s, jn], (iw, peer))
            )
        for copy in started:
            copy.start()
        return started

    offset = lax.rem(jn * z_own, LANES)
    spread = (
        lax.rem(lax.broadcasted_iota(jnp.int32, (LANES, y_all), 0), y_all)
        == lax.broadcasted_iota(jnp.int32, (LANES, y_all), 1)
    ).astype(jnp.bfloat16)
    z_id = lax.broadcasted_iota(jnp.int32, (LANES, LANES), 1) - offset
    k_id = lax.broadcasted_iota(jnp.int32, (LANES, LANES), 0) // y_all
    fits = lax.rem(z_id + LANES, z_group) == k_id
    pick_row = lax.broadcasted_iota(jnp.int32, (16 * groups, LANES), 0)
    pick_z = lax.broadcasted_iota(jnp.int32, (16 * groups, LANES), 1) - offset
    inside = (pick_z >= 0) & (pick_z // z_group == pick_row // 16)

    def order_snapshot(s):
        for d in range(1, narrow):
            peer = n_peer(d)
            remote(packed.at[s + 1, 0], snap_in.at[s, peer], snap_send.at[s, d], snap_recv.at[s, peer], (iw, peer)).wait_recv()
        arrived = [snap_in[s, n].astype(jnp.float32) for n in range(narrow)]
        pick = (inside & (lax.rem(pick_row, 16) == 16 - stages + s)).astype(jnp.bfloat16)
        for c in range(comps):
            cells = jnp.concatenate([a[c * cells_y : (c + 1) * cells_y, :] for a in arrived], 0)
            wide_cells = jnp.dot(spread, cells.astype(jnp.bfloat16), preferred_element_type=jnp.float32)
            chosen = jnp.where(fits, wide_cells, 0.0).astype(jnp.bfloat16)
            ordered = lax.dot_general(pick, chosen, NT, preferred_element_type=jnp.float32)
            flat = jnp.concatenate([ordered[16 * g : 16 * g + 16, :] for g in range(groups)], 1)
            tail[c] = (tail[c].astype(jnp.float32) + flat).astype(jnp.bfloat16)

    tiles, pivots = [], []
    inverse_cells = 1.0 / (wide * narrow * cells_y * cells_z)

    def begin():
        for t in range(columns // 8):
            rows = whole[(8 * t) // piece_rows, (8 * t) % piece_rows : (8 * t) % piece_rows + 8, :]
            tiles.append(rows * inverse_cells)

    def run(start, stop):
        for p in range(start, stop):
            pivots.append(eliminate_panel(tiles, p, 0, min(8, prior - 8 * p)))

    row = lax.broadcasted_iota(jnp.int32, (cells_y, cells_z), 0)
    base = current
    for s in range(stages):
        for copy in copies:
            copy.wait_recv()
        x_low = unpack(x_halo.at[s, 0])
        x_high = unpack(x_halo.at[s, 1])
        y_low, y_high = [], []
        for c in range(comps):
            low = jnp.broadcast_to(y_halo[s, 0, c : c + 1, :], (cells_y, cells_z))
            high = jnp.broadcast_to(y_halo[s, 1, c : c + 1, :], (cells_y, cells_z))
            y_low.append(jnp.where(row == 0, low, pltpu.roll(current[c], 1, 0)))
            y_high.append(jnp.where(row == cells_y - 1, high, pltpu.roll(current[c], cells_y - 1, 0)))
        change = tendency(current, x_low, x_high, y_low, y_high)
        moved = [a + TIME_STEP * b for a, b in zip(current, change)]
        if s % 2 == 1:
            moved = [0.5 * a + 0.5 * b for a, b in zip(base, moved)]
            base = moved
        current = moved
        put_state(s + 1, current)
        if s + 1 < stages:
            copies = halo_copies(s + 1)
            for copy in copies:
                copy.start()
            pending += copies
        pending += send_snapshot(s)
        if s == 0:
            pending += reduce_step(1)
            pending += reduce_step(2)
        if s == 1:
            reduce_step(3)
            begin()
            run(0, 3)
        if s == 2:
            run(3, 6)
        if s > 0:
            order_snapshot(s - 1)
    for c in range(comps):
        flow[c] = current[c]

    run(6, 9)
    order_snapshot(stages - 1)
    total = jnp.zeros((16, columns), jnp.float32)
    for c in range(comps):
        rows = tail[c]
        x = jnp.concatenate([modes[c, 0:keep, :], rows], 0)
        total = total + lax.dot_general(rows, x, NT, preferred_element_type=jnp.float32)
    mine8 = total[8:16, :]
    rows8[...] = mine8
    rows_n[jn] = mine8
    started = [
        remote(rows8, rows_n.at[jn], last_send.at[0, d], last_recv.at[0, jn], (iw, n_peer(d)))
        for d in range(1, narrow)
    ]
    for copy in started:
        copy.start()
    pending += started
    run(9, 12)
    for d in range(1, narrow):
        peer = n_peer(d)
        remote(rows8, rows_n.at[peer], last_send.at[0, d], last_recv.at[0, peer], (iw, peer)).wait_recv()
    sum8 = rows_n[0]
    for n in range(1, narrow):
        sum8 = sum8 + rows_n[n]
    sums8[...] = sum8
    rows_w[iw] = sum8
    started = [
        remote(sums8, rows_w.at[iw], last_send.at[1, d], last_recv.at[1, iw], (w_peer(d), jn))
        for d in range(1, wide)
    ]
    for copy in started:
        copy.start()
    pending += started
    run(12, columns // 8)
    lane, row = lane_ids(), row_ids()
    uppers, inverse = [], []
    for t in range(columns // 8):
        scale = lax.rsqrt(jnp.where(pivots[t] > 0.0, pivots[t], 1.0))
        scale = jnp.where(row + 8 * t < prior, scale, 0.0)
        uppers.append(jnp.where(lane >= row + 8 * t, tiles[t], 0.0) * scale)
        left = jnp.where(lane < row + 8 * t, tiles[t], 0.0)
        inverse.append(jnp.where(lane == row + 8 * t, 1.0, left) * scale)
    inverse = jnp.concatenate(inverse, 0)
    for copy in pending:
        copy.wait_send()
    for d in range(1, wide):
        peer = w_peer(d)
        remote(sums8, rows_w.at[peer], last_send.at[1, d], last_recv.at[1, peer], (peer, jn)).wait_recv()
    sum8 = rows_w[0]
    for w in range(1, wide):
        sum8 = sum8 + rows_w[w]

    exact = lax.Precision.HIGHEST
    corner = row + columns - 8 >= prior
    rows = jnp.where(corner, sum8 * inverse_cells, 0.0)
    known = jnp.where(lane < prior, rows, 0.0)
    solved = lax.dot_general(known, inverse, NT, precision=exact, preferred_element_type=jnp.float32)
    bottom = jnp.concatenate([jnp.zeros((columns - 8, columns), jnp.float32), solved], 0)
    taken = lax.dot_general(solved, bottom, NT, precision=exact, preferred_element_type=jnp.float32)
    last_tile = [jnp.where(lane >= prior, rows - taken, 0.0)]
    last_tile = [pltpu.roll(last_tile[0], 8, 1)]
    left = eliminate_panel(last_tile, 0, prior - (columns - 8), 8)
    tip = jnp.where(lane >= row, last_tile[0], 0.0) * lax.rsqrt(jnp.where(corner, left, 1.0))
    tip = pltpu.roll(jnp.where(corner, tip, 0.0), LANES - 8, 1)
    side = jnp.transpose(bottom)
    for t in range(columns // 8):
        out = uppers[t] + side[8 * t : 8 * t + 8, :]
        if t == columns // 8 - 1:
            out = jnp.where(corner, tip, out)
        factor_out[8 * t : 8 * t + 8, :] = out


def local(wide, narrow, fields, prior_modes):
    comps, cells_x, cells_y, cells_z = fields.shape
    prior = prior_modes.shape[0]
    stages = 2 * STEPS
    columns = prior + stages
    modes = jnp.transpose(prior_modes, (1, 2, 0, 3)).reshape(comps, prior, prior_modes.shape[3])
    piece = columns // wide
    snap_rows = -(-comps * cells_y // 16) * 16
    f32, bf16 = jnp.float32, jnp.bfloat16
    vmem = pl.BlockSpec(memory_space=pltpu.VMEM)
    dma = pltpu.SemaphoreType.DMA
    flow, factor = pl.pallas_call(
        functools.partial(kernel, wide, narrow),
        out_shape=(
            jax.ShapeDtypeStruct((comps, cells_y, cells_z), f32),
            jax.ShapeDtypeStruct((columns, columns), f32),
        ),
        in_specs=[pl.BlockSpec(memory_space=pltpu.HBM)] * 2,
        out_specs=(vmem, vmem),
        scratch_shapes=[
            pltpu.VMEM(modes.shape, bf16), dma((comps,)),
            pltpu.VMEM((comps, cells_y, cells_z), f32), dma((1,)),
            pltpu.VMEM((stages + 1, cells_z // LANES, snap_rows, LANES), bf16),
            pltpu.VMEM((stages, 2, cells_z // LANES, snap_rows, LANES), bf16),
            pltpu.VMEM((stages, 2, 8, cells_z), f32),
            pltpu.VMEM((stages, 2, 8, cells_z), f32),
            dma((stages, 4)), dma((stages, 4)),
            pltpu.VMEM((stages, narrow, snap_rows, LANES), bf16),
            dma((stages, narrow)), dma((stages, narrow)),
            pltpu.VMEM((columns, columns), f32),
            pltpu.VMEM((wide, piece, columns), f32),
            pltpu.VMEM((piece, columns), f32),
            pltpu.VMEM((narrow, piece, columns), f32),
            pltpu.VMEM((wide, piece, columns), f32),
            pltpu.VMEM((piece, columns), f32),
            dma((3, max(wide, narrow))), dma((3, max(wide, narrow))),
            pltpu.VMEM((comps, 16, modes.shape[2]), bf16),
            pltpu.VMEM((8, columns), f32),
            pltpu.VMEM((narrow, 8, columns), f32),
            pltpu.VMEM((8, columns), f32),
            pltpu.VMEM((wide, 8, columns), f32),
            dma((2, max(wide, narrow))), dma((2, max(wide, narrow))),
        ],
        compiler_params=pltpu.CompilerParams(
            collective_id=0, has_side_effects=True, vmem_limit_bytes=52 * 1024 * 1024
        ),
    )(fields.reshape(comps, cells_y, cells_z), modes)
    return flow.reshape(fields.shape), factor


def solution(mesh):
    wide, narrow = mesh.shape["wide"], mesh.shape["narrow"]
    return jax.shard_map(
        functools.partial(local, wide, narrow),
        mesh=mesh,
        in_specs=(P(None, "wide", "narrow", None), P(None, None, "wide", "narrow")),
        out_specs=(P(None, "wide", "narrow", None), P()),
        check_vma=False,
    )
```

```python
import functools

import jax
import jax.numpy as jnp
from jax import lax
from jax.experimental import pallas as pl
from jax.experimental.pallas import tpu as pltpu
from jax.sharding import PartitionSpec as P

STEPS = 2
GAMMA = 1.4
TIME_STEP = 0.25
VISCOSITY = 0.15
LANES = 128
NT = (((1,), (1,)), ((), ()))


def flux_of(state, d):
    density, energy = state[0], state[4]
    momentum = state[1:4]
    inverse = 1.0 / density
    vel = momentum[d] * inverse
    squares = momentum[0] * momentum[0] + momentum[1] * momentum[1] + momentum[2] * momentum[2]
    pressure = (GAMMA - 1.0) * (energy - 0.5 * squares * inverse)
    out = [momentum[d], momentum[0] * vel, momentum[1] * vel, momentum[2] * vel]
    out.append((energy + pressure) * vel)
    out[1 + d] = out[1 + d] + pressure
    return out


def tendency(here, x_low, x_high, y_low, y_high):
    cells_z = here[0].shape[1]
    z_low = [pltpu.roll(c, 1, 1) for c in here]
    z_high = [pltpu.roll(c, cells_z - 1, 1) for c in here]
    total = None
    for d, (low, high) in enumerate(((x_low, x_high), (y_low, y_high), (z_low, z_high))):
        flux_low, flux_high = flux_of(low, d), flux_of(high, d)
        part = [
            -0.5 * (fh - fl) + VISCOSITY * (l + h)
            for fh, fl, l, h in zip(flux_high, flux_low, low, high)
        ]
        total = part if total is None else [a + b for a, b in zip(total, part)]
    return [t - (6.0 * VISCOSITY) * c for t, c in zip(total, here)]


def lane_ids():
    return lax.broadcasted_iota(jnp.int32, (8, LANES), 1)


def row_ids():
    return lax.broadcasted_iota(jnp.int32, (8, LANES), 0)


def column_of(tile, j):
    return jnp.broadcast_to(tile[:, j : j + 1], (8, LANES))


def row_of(tile, k):
    return jnp.broadcast_to(tile[k : k + 1, :], (8, LANES))


def inverted(x):
    guess = pl.reciprocal(x, approx=True)
    guess = guess * (2.0 - x * guess)
    return guess * (2.0 - x * guess)


def eliminate_panel(tiles, p, first, last):
    lane, row = lane_ids(), row_ids()
    pivots = jnp.zeros((8, LANES), jnp.float32)
    steps = range(first, last)
    panel = tiles[p]
    columns = {k: column_of(panel, 8 * p + k) for k in steps}
    heads, inverses, crossings = {}, {}, {}
    for k in steps:
        j = 8 * p + k
        pivot = row_of(columns[k], k)
        inverses[k] = inverted(pivot)
        pivots = jnp.where(row == k, pivot, pivots)
        factor = jnp.where(row > k, columns[k], 0.0) * inverses[k]
        for m in steps:
            if m > k:
                crossings[k, m] = row_of(columns[m], k)
                columns[m] = columns[m] - factor * crossings[k, m]
        heads[k] = jnp.where(lane == j, 1.0, row_of(panel, k))
        panel = jnp.where((lane == j) & (row > k), 0.0, panel) - factor * heads[k]
    tiles[p] = panel
    cleared = (lane >= 8 * p + first) & (lane < 8 * p + last)
    for t in range(p + 1, len(tiles)):
        columns = {k: column_of(tiles[t], 8 * p + k) for k in steps}
        rest = jnp.where(cleared, 0.0, tiles[t])
        for k in steps:
            factor = columns[k] * inverses[k]
            for m in steps:
                if m > k:
                    columns[m] = columns[m] - factor * crossings[k, m]
            outside = jnp.where((lane > 8 * p + k) & cleared, 0.0, heads[k])
            rest = rest - factor * outside
        tiles[t] = rest
    return pivots


def kernel(
    wide, narrow, fields, modes_hbm, flow, factor_out,
    modes, modes_sem, start, start_sem, packed, x_halo, y_send, y_halo, halo_send, halo_recv,
    snap_in, snap_send, snap_recv,
    gram, scatter, part, share, whole, piece, red_send, red_recv,
    tail, rows8, rows_n, sums8, rows_w, last_send, last_recv,
):
    stages = 2 * STEPS
    comps, cells_y, cells_z = fields.shape
    prior = modes.shape[1]
    columns = gram.shape[0]
    mode_lanes = modes.shape[2]
    y_all = cells_y * narrow
    z_own = cells_z // narrow
    z_group = LANES // y_all
    groups = mode_lanes // LANES
    piece_rows = columns // wide
    keep = columns - 16
    iw, jn = lax.axis_index("wide"), lax.axis_index("narrow")

    def w_peer(d):
        return lax.rem(iw + d, wide)

    def n_peer(d):
        return lax.rem(jn + d, narrow)

    def remote(src, dst, send, recv, device):
        return pltpu.make_async_remote_copy(
            src_ref=src, dst_ref=dst, send_sem=send, recv_sem=recv,
            device_id=device, device_id_type=pl.DeviceIdType.MESH,
        )

    loads = [pltpu.make_async_copy(modes_hbm.at[c], modes.at[c], modes_sem.at[c]) for c in range(comps)]
    fields_load = pltpu.make_async_copy(fields, start, start_sem.at[0])
    fields_load.start()
    for load in loads:
        load.start()

    barrier = pltpu.get_barrier_semaphore()
    for d in range(1, wide):
        pl.semaphore_signal(barrier, inc=1, device_id=(w_peer(d), jn), device_id_type=pl.DeviceIdType.MESH)
    for d in range(1, narrow):
        pl.semaphore_signal(barrier, inc=1, device_id=(iw, n_peer(d)), device_id_type=pl.DeviceIdType.MESH)

    def halo_copies(s):
        right, left = (w_peer(1), jn), (w_peer(wide - 1), jn)
        up, down = (iw, n_peer(1)), (iw, n_peer(narrow - 1))
        return [
            remote(packed.at[s], x_halo.at[s, 0], halo_send.at[s, 0], halo_recv.at[s, 0], right),
            remote(packed.at[s], x_halo.at[s, 1], halo_send.at[s, 1], halo_recv.at[s, 1], left),
            remote(y_send.at[s, 1], y_halo.at[s, 0], halo_send.at[s, 2], halo_recv.at[s, 2], up),
            remote(y_send.at[s, 0], y_halo.at[s, 1], halo_send.at[s, 3], halo_recv.at[s, 3], down),
        ]

    def put_state(s, values):
        spare = jnp.zeros((packed.shape[2] - comps * cells_y, cells_z), jnp.float32)
        stacked = jnp.concatenate(values + [spare], 0).astype(jnp.bfloat16)
        for b in range(cells_z // LANES):
            packed[s, b] = stacked[:, b * LANES : (b + 1) * LANES]
        if s < stages:
            for c in range(comps):
                y_send[s, 0, c : c + 1, :] = values[c][0:1, :]
                y_send[s, 1, c : c + 1, :] = values[c][cells_y - 1 : cells_y, :]
            for c in range(comps, 8):
                y_send[s, 0, c : c + 1, :] = jnp.zeros((1, cells_z), jnp.float32)
                y_send[s, 1, c : c + 1, :] = jnp.zeros((1, cells_z), jnp.float32)

    def unpack(ref):
        blocks = [ref[b].astype(jnp.float32) for b in range(cells_z // LANES)]
        return [
            jnp.concatenate([x[c * cells_y : (c + 1) * cells_y, :] for x in blocks], 1)
            for c in range(comps)
        ]

    fields_load.wait()
    current = [start[c] for c in range(comps)]
    put_state(0, current)
    def gram_part(c):
        loads[c].wait()
        last = modes[c, keep:prior, :].astype(jnp.float32)
        last = jnp.concatenate([last, jnp.zeros((columns - prior, mode_lanes), jnp.float32)], 0)
        tail[c] = last.astype(jnp.bfloat16)
        x = jnp.concatenate([modes[c, 0:keep, :], tail[c]], 0)
        return lax.dot_general(x, x, NT, preferred_element_type=jnp.float32)

    total = gram_part(0)
    pl.semaphore_wait(barrier, wide + narrow - 2)

    copies = halo_copies(0)
    for copy in copies:
        copy.start()
    pending = list(copies)

    for c in range(1, comps):
        total = total + gram_part(c)
    gram[...] = total
    mine = pl.ds(pl.multiple_of(iw * piece_rows, piece_rows), piece_rows)
    scatter[iw] = gram[mine, :]
    first = []
    for d in range(1, wide):
        peer = w_peer(d)
        theirs = pl.ds(pl.multiple_of(peer * piece_rows, piece_rows), piece_rows)
        first.append(remote(gram.at[theirs], scatter.at[iw], red_send.at[0, d], red_recv.at[0, iw], (peer, jn)))
    for copy in first:
        copy.start()
    pending += first

    def reduce_step(s):
        started = []
        if s == 1:
            for d in range(1, wide):
                peer = w_peer(d)
                remote(gram.at[mine], scatter.at[peer], red_send.at[0, d], red_recv.at[0, peer], (peer, jn)).wait_recv()
            acc = scatter[0]
            for w in range(1, wide):
                acc = acc + scatter[w]
            part[...] = acc
            share[jn] = acc
            for d in range(1, narrow):
                started.append(remote(part, share.at[jn], red_send.at[1, d], red_recv.at[1, jn], (iw, n_peer(d))))
        elif s == 2:
            for d in range(1, narrow):
                peer = n_peer(d)
                remote(part, share.at[peer], red_send.at[1, d], red_recv.at[1, peer], (iw, peer)).wait_recv()
            acc = share[0]
            for n in range(1, narrow):
                acc = acc + share[n]
            piece[...] = acc
            whole[iw] = acc
            for d in range(1, wide):
                started.append(remote(piece, whole.at[iw], red_send.at[2, d], red_recv.at[2, iw], (w_peer(d), jn)))
        elif s == 3:
            for d in range(1, wide):
                peer = w_peer(d)
                remote(piece, whole.at[peer], red_send.at[2, d], red_recv.at[2, peer], (peer, jn)).wait_recv()
        for copy in started:
            copy.start()
        return started

    def send_snapshot(s):
        snap_in[s, jn] = packed[s + 1, (jn * z_own) // LANES]
        started = []
        for d in range(1, narrow):
            peer = n_peer(d)
            started.append(
                remote(packed.at[s + 1, (peer * z_own) // LANES], snap_in.at[s, jn],
                       snap_send.at[s, d], snap_recv.at[s, jn], (iw, peer))
            )
        for copy in started:
            copy.start()
        return started

    offset = lax.rem(jn * z_own, LANES)
    spread = (
        lax.rem(lax.broadcasted_iota(jnp.int32, (y_all, LANES), 1), y_all)
        == lax.broadcasted_iota(jnp.int32, (y_all, LANES), 0)
    ).astype(jnp.bfloat16)
    z_id = lax.broadcasted_iota(jnp.int32, (LANES, LANES), 0) - offset
    k_id = lax.broadcasted_iota(jnp.int32, (LANES, LANES), 1) // y_all
    fits = lax.rem(z_id + LANES, z_group) == k_id
    pick_row = lax.broadcasted_iota(jnp.int32, (16 * groups, LANES), 0)
    pick_z = lax.broadcasted_iota(jnp.int32, (16 * groups, LANES), 1) - offset
    inside = (pick_z >= 0) & (pick_z // z_group == pick_row // 16)

    def order_snapshot(s):
        for d in range(1, narrow):
            peer = n_peer(d)
            remote(packed.at[s + 1, 0], snap_in.at[s, peer], snap_send.at[s, d], snap_recv.at[s, peer], (iw, peer)).wait_recv()
        arrived = [snap_in[s, n].astype(jnp.float32) for n in range(narrow)]
        pick = (inside & (lax.rem(pick_row, 16) == 16 - stages + s)).astype(jnp.bfloat16)
        for c in range(comps):
            cells = jnp.concatenate([a[c * cells_y : (c + 1) * cells_y, :] for a in arrived], 0)
            wide_cells = lax.dot_general(
                cells.astype(jnp.bfloat16), spread, (((0,), (0,)), ((), ())), preferred_element_type=jnp.float32
            )
            chosen = jnp.where(fits, wide_cells, 0.0).astype(jnp.bfloat16)
            ordered = jnp.dot(pick, chosen, preferred_element_type=jnp.float32)
            flat = jnp.concatenate([ordered[16 * g : 16 * g + 16, :] for g in range(groups)], 1)
            tail[c] = (tail[c].astype(jnp.float32) + flat).astype(jnp.bfloat16)

    tiles, pivots = [], []
    inverse_cells = 1.0 / (wide * narrow * cells_y * cells_z)

    def begin():
        for t in range(columns // 8):
            rows = whole[(8 * t) // piece_rows, (8 * t) % piece_rows : (8 * t) % piece_rows + 8, :]
            tiles.append(rows * inverse_cells)

    def run(start, stop):
        for p in range(start, stop):
            pivots.append(eliminate_panel(tiles, p, 0, min(8, prior - 8 * p)))

    row = lax.broadcasted_iota(jnp.int32, (cells_y, cells_z), 0)
    base = current
    for s in range(stages):
        for copy in copies:
            copy.wait_recv()
        x_low = unpack(x_halo.at[s, 0])
        x_high = unpack(x_halo.at[s, 1])
        y_low, y_high = [], []
        for c in range(comps):
            low = jnp.broadcast_to(y_halo[s, 0, c : c + 1, :], (cells_y, cells_z))
            high = jnp.broadcast_to(y_halo[s, 1, c : c + 1, :], (cells_y, cells_z))
            y_low.append(jnp.where(row == 0, low, pltpu.roll(current[c], 1, 0)))
            y_high.append(jnp.where(row == cells_y - 1, high, pltpu.roll(current[c], cells_y - 1, 0)))
        change = tendency(current, x_low, x_high, y_low, y_high)
        moved = [a + TIME_STEP * b for a, b in zip(current, change)]
        if s % 2 == 1:
            moved = [0.5 * a + 0.5 * b for a, b in zip(base, moved)]
            base = moved
        current = moved
        put_state(s + 1, current)
        if s + 1 < stages:
            copies = halo_copies(s + 1)
            for copy in copies:
                copy.start()
            pending += copies
        pending += send_snapshot(s)
        pending += reduce_step(s + 1)
        if s > 0:
            order_snapshot(s - 1)
        if s == stages - 2:
            begin()
            run(0, 4)
    for c in range(comps):
        flow[c] = current[c]

    run(4, 8)
    order_snapshot(stages - 1)
    total = jnp.zeros((columns, 16), jnp.float32)
    for c in range(comps):
        rows = tail[c]
        x = jnp.concatenate([modes[c, 0:keep, :], rows], 0)
        total = total + lax.dot_general(x, rows, NT, preferred_element_type=jnp.float32)
    mine8 = jnp.transpose(total)[8:16, :]
    rows8[...] = mine8
    rows_n[jn] = mine8
    started = [
        remote(rows8, rows_n.at[jn], last_send.at[0, d], last_recv.at[0, jn], (iw, n_peer(d)))
        for d in range(1, narrow)
    ]
    for copy in started:
        copy.start()
    pending += started
    run(8, 12)
    for d in range(1, narrow):
        peer = n_peer(d)
        remote(rows8, rows_n.at[peer], last_send.at[0, d], last_recv.at[0, peer], (iw, peer)).wait_recv()
    sum8 = rows_n[0]
    for n in range(1, narrow):
        sum8 = sum8 + rows_n[n]
    sums8[...] = sum8
    rows_w[iw] = sum8
    started = [
        remote(sums8, rows_w.at[iw], last_send.at[1, d], last_recv.at[1, iw], (w_peer(d), jn))
        for d in range(1, wide)
    ]
    for copy in started:
        copy.start()
    pending += started
    run(12, columns // 8)
    lane, row = lane_ids(), row_ids()
    uppers, inverse = [], []
    for t in range(columns // 8):
        scale = lax.rsqrt(jnp.where(pivots[t] > 0.0, pivots[t], 1.0))
        scale = jnp.where(row + 8 * t < prior, scale, 0.0)
        uppers.append(jnp.where(lane >= row + 8 * t, tiles[t], 0.0) * scale)
        left = jnp.where(lane < row + 8 * t, tiles[t], 0.0)
        inverse.append(jnp.where(lane == row + 8 * t, 1.0, left) * scale)
    inverse = jnp.concatenate(inverse, 0)
    for copy in pending:
        copy.wait_send()
    for d in range(1, wide):
        peer = w_peer(d)
        remote(sums8, rows_w.at[peer], last_send.at[1, d], last_recv.at[1, peer], (peer, jn)).wait_recv()
    sum8 = rows_w[0]
    for w in range(1, wide):
        sum8 = sum8 + rows_w[w]

    exact = lax.Precision.HIGHEST
    corner = row + columns - 8 >= prior
    rows = jnp.where(corner, sum8 * inverse_cells, 0.0)
    known = jnp.where(lane < prior, rows, 0.0)
    solved = lax.dot_general(known, inverse, NT, precision=exact, preferred_element_type=jnp.float32)
    bottom = jnp.concatenate([jnp.zeros((columns - 8, columns), jnp.float32), solved], 0)
    taken = lax.dot_general(solved, bottom, NT, precision=exact, preferred_element_type=jnp.float32)
    last_tile = [jnp.where(lane >= prior, rows - taken, 0.0)]
    last_tile = [pltpu.roll(last_tile[0], 8, 1)]
    left = eliminate_panel(last_tile, 0, prior - (columns - 8), 8)
    tip = jnp.where(lane >= row, last_tile[0], 0.0) * lax.rsqrt(jnp.where(corner, left, 1.0))
    tip = pltpu.roll(jnp.where(corner, tip, 0.0), LANES - 8, 1)
    side = jnp.transpose(bottom)
    for t in range(columns // 8):
        out = uppers[t] + side[8 * t : 8 * t + 8, :]
        if t == columns // 8 - 1:
            out = jnp.where(corner, tip, out)
        factor_out[8 * t : 8 * t + 8, :] = out


def local(wide, narrow, fields, prior_modes):
    comps, cells_x, cells_y, cells_z = fields.shape
    prior = prior_modes.shape[0]
    stages = 2 * STEPS
    columns = prior + stages
    modes = jnp.transpose(prior_modes, (1, 2, 0, 3)).reshape(comps, prior, prior_modes.shape[3])
    piece = columns // wide
    snap_rows = -(-comps * cells_y // 16) * 16
    f32, bf16 = jnp.float32, jnp.bfloat16
    vmem = pl.BlockSpec(memory_space=pltpu.VMEM)
    dma = pltpu.SemaphoreType.DMA
    flow, factor = pl.pallas_call(
        functools.partial(kernel, wide, narrow),
        out_shape=(
            jax.ShapeDtypeStruct((comps, cells_y, cells_z), f32),
            jax.ShapeDtypeStruct((columns, columns), f32),
        ),
        in_specs=[pl.BlockSpec(memory_space=pltpu.HBM)] * 2,
        out_specs=(vmem, vmem),
        scratch_shapes=[
            pltpu.VMEM(modes.shape, bf16), dma((comps,)),
            pltpu.VMEM((comps, cells_y, cells_z), f32), dma((1,)),
            pltpu.VMEM((stages + 1, cells_z // LANES, snap_rows, LANES), bf16),
            pltpu.VMEM((stages, 2, cells_z // LANES, snap_rows, LANES), bf16),
            pltpu.VMEM((stages, 2, 8, cells_z), f32),
            pltpu.VMEM((stages, 2, 8, cells_z), f32),
            dma((stages, 4)), dma((stages, 4)),
            pltpu.VMEM((stages, narrow, snap_rows, LANES), bf16),
            dma((stages, narrow)), dma((stages, narrow)),
            pltpu.VMEM((columns, columns), f32),
            pltpu.VMEM((wide, piece, columns), f32),
            pltpu.VMEM((piece, columns), f32),
            pltpu.VMEM((narrow, piece, columns), f32),
            pltpu.VMEM((wide, piece, columns), f32),
            pltpu.VMEM((piece, columns), f32),
            dma((3, max(wide, narrow))), dma((3, max(wide, narrow))),
            pltpu.VMEM((comps, 16, modes.shape[2]), bf16),
            pltpu.VMEM((8, columns), f32),
            pltpu.VMEM((narrow, 8, columns), f32),
            pltpu.VMEM((8, columns), f32),
            pltpu.VMEM((wide, 8, columns), f32),
            dma((2, max(wide, narrow))), dma((2, max(wide, narrow))),
        ],
        compiler_params=pltpu.CompilerParams(
            collective_id=0, has_side_effects=True, vmem_limit_bytes=52 * 1024 * 1024
        ),
    )(fields.reshape(comps, cells_y, cells_z), modes)
    return flow.reshape(fields.shape), factor


def solution(mesh):
    wide, narrow = mesh.shape["wide"], mesh.shape["narrow"]
    return jax.shard_map(
        functools.partial(local, wide, narrow),
        mesh=mesh,
        in_specs=(P(None, "wide", "narrow", None), P(None, None, "wide", "narrow")),
        out_specs=(P(None, "wide", "narrow", None), P()),
        check_vma=False,
    )
```

```python
import functools

import jax
import jax.numpy as jnp
from jax import lax
from jax.experimental import pallas as pl
from jax.experimental.pallas import tpu as pltpu
from jax.sharding import PartitionSpec as P

STEPS = 2
GAMMA = 1.4
TIME_STEP = 0.25
VISCOSITY = 0.15
LANES = 128
NT = (((1,), (1,)), ((), ()))


def flux_of(state, d):
    density, energy = state[0], state[4]
    momentum = state[1:4]
    inverse = 1.0 / density
    vel = momentum[d] * inverse
    squares = momentum[0] * momentum[0] + momentum[1] * momentum[1] + momentum[2] * momentum[2]
    pressure = (GAMMA - 1.0) * (energy - 0.5 * squares * inverse)
    out = [momentum[d], momentum[0] * vel, momentum[1] * vel, momentum[2] * vel]
    out.append((energy + pressure) * vel)
    out[1 + d] = out[1 + d] + pressure
    return out


def along(low, high, d):
    return [
        -0.5 * (fh - fl) + VISCOSITY * (l + h)
        for fh, fl, l, h in zip(flux_of(high, d), flux_of(low, d), low, high)
    ]


def inner_part(here):
    cells_z = here[0].shape[1]
    z_low = [pltpu.roll(c, 1, 1) for c in here]
    z_high = [pltpu.roll(c, cells_z - 1, 1) for c in here]
    return [a - (6.0 * VISCOSITY) * c for a, c in zip(along(z_low, z_high, 2), here)]


def lane_ids():
    return lax.broadcasted_iota(jnp.int32, (8, LANES), 1)


def row_ids():
    return lax.broadcasted_iota(jnp.int32, (8, LANES), 0)


def column_of(tile, j):
    return jnp.broadcast_to(tile[:, j : j + 1], (8, LANES))


def row_of(tile, k):
    return jnp.broadcast_to(tile[k : k + 1, :], (8, LANES))


def inverted(x):
    guess = pl.reciprocal(x, approx=True)
    guess = guess * (2.0 - x * guess)
    return guess * (2.0 - x * guess)


def eliminate_panel(tiles, p, first, last):
    lane, row = lane_ids(), row_ids()
    steps = range(first, last)
    panel = tiles[p]
    inside = (lane >= 8 * p + first) & (lane < 8 * p + last)
    spread = {k: column_of(panel, 8 * p + k) for k in steps}
    entry = {(m, k): row_of(spread[k], m) for k in steps for m in range(k, last)}
    inverses, ratio = {}, {}
    for k in steps:
        inverses[k] = inverted(entry[k, k])
        for m in range(k + 1, last):
            ratio[m, k] = entry[m, k] * inverses[k]
            for n in range(m, last):
                entry[n, m] = entry[n, m] - entry[n, k] * ratio[m, k]
    raw = {k: row_of(panel, k) for k in steps}
    heads = {k: jnp.where(inside, jnp.where(lane == 8 * p + k, 1.0, 0.0), raw[k]) for k in steps}
    for k in steps:
        for m in range(first, k):
            raw[k] = raw[k] - ratio[k, m] * raw[m]
            heads[k] = heads[k] - ratio[k, m] * heads[m]
    pivots = jnp.zeros((8, LANES), jnp.float32)
    panel = jnp.zeros((8, LANES), jnp.float32)
    for k in steps:
        pivots = jnp.where(row == k, entry[k, k], pivots)
        panel = jnp.where(row == k, jnp.where(inside & (lane < 8 * p + k), heads[k], raw[k]), panel)
    tiles[p] = panel
    for t in range(p + 1, len(tiles)):
        rest = jnp.where(inside, 0.0, tiles[t])
        factors = {}
        for k in steps:
            left = column_of(tiles[t], 8 * p + k)
            for m in range(first, k):
                left = left - factors[m] * entry[k, m]
            factors[k] = left * inverses[k]
            rest = rest - factors[k] * heads[k]
        tiles[t] = rest
    return pivots


def kernel(
    wide, narrow, fields, modes_hbm, flow, factor_out,
    modes, modes_sem, start, start_sem, packed, x_halo, y_send, y_halo, halo_send, halo_recv,
    snap_in, snap_send, snap_recv,
    gram, scatter, part, share, whole, piece, red_send, red_recv,
    tail, rows8, rows_n, sums8, rows_w, last_send, last_recv,
):
    stages = 2 * STEPS
    comps, cells_y, cells_z = fields.shape
    prior = modes.shape[1]
    columns = gram.shape[0]
    mode_lanes = modes.shape[2]
    y_all = cells_y * narrow
    z_own = cells_z // narrow
    z_group = LANES // y_all
    groups = mode_lanes // LANES
    piece_rows = columns // wide
    keep = columns - 16
    iw, jn = lax.axis_index("wide"), lax.axis_index("narrow")

    def w_peer(d):
        return lax.rem(iw + d, wide)

    def n_peer(d):
        return lax.rem(jn + d, narrow)

    def remote(src, dst, send, recv, device):
        return pltpu.make_async_remote_copy(
            src_ref=src, dst_ref=dst, send_sem=send, recv_sem=recv,
            device_id=device, device_id_type=pl.DeviceIdType.MESH,
        )

    loads = [pltpu.make_async_copy(modes_hbm.at[c], modes.at[c], modes_sem.at[c]) for c in range(comps)]
    fields_load = pltpu.make_async_copy(fields, start, start_sem.at[0])
    fields_load.start()
    for load in loads:
        load.start()

    barrier = pltpu.get_barrier_semaphore()
    for d in range(1, wide):
        pl.semaphore_signal(barrier, inc=1, device_id=(w_peer(d), jn), device_id_type=pl.DeviceIdType.MESH)
    for d in range(1, narrow):
        pl.semaphore_signal(barrier, inc=1, device_id=(iw, n_peer(d)), device_id_type=pl.DeviceIdType.MESH)

    def halo_copies(s):
        right, left = (w_peer(1), jn), (w_peer(wide - 1), jn)
        up, down = (iw, n_peer(1)), (iw, n_peer(narrow - 1))
        return [
            remote(packed.at[s], x_halo.at[s, 0], halo_send.at[s, 0], halo_recv.at[s, 0], right),
            remote(packed.at[s], x_halo.at[s, 1], halo_send.at[s, 1], halo_recv.at[s, 1], left),
            remote(y_send.at[s, 1], y_halo.at[s, 0], halo_send.at[s, 2], halo_recv.at[s, 2], up),
            remote(y_send.at[s, 0], y_halo.at[s, 1], halo_send.at[s, 3], halo_recv.at[s, 3], down),
        ]

    def put_state(s, values):
        spare = jnp.zeros((packed.shape[2] - comps * cells_y, cells_z), jnp.float32)
        stacked = jnp.concatenate(values + [spare], 0).astype(jnp.bfloat16)
        for b in range(cells_z // LANES):
            packed[s, b] = stacked[:, b * LANES : (b + 1) * LANES]
        if s < stages:
            for c in range(comps):
                y_send[s, 0, c : c + 1, :] = values[c][0:1, :]
                y_send[s, 1, c : c + 1, :] = values[c][cells_y - 1 : cells_y, :]
            for c in range(comps, 8):
                y_send[s, 0, c : c + 1, :] = jnp.zeros((1, cells_z), jnp.float32)
                y_send[s, 1, c : c + 1, :] = jnp.zeros((1, cells_z), jnp.float32)

    def unpack(ref):
        blocks = [ref[b].astype(jnp.float32) for b in range(cells_z // LANES)]
        return [
            jnp.concatenate([x[c * cells_y : (c + 1) * cells_y, :] for x in blocks], 1)
            for c in range(comps)
        ]

    fields_load.wait()
    current = [start[c] for c in range(comps)]
    put_state(0, current)
    def gram_part(c):
        loads[c].wait()
        last = modes[c, keep:prior, :].astype(jnp.float32)
        last = jnp.concatenate([last, jnp.zeros((columns - prior, mode_lanes), jnp.float32)], 0)
        tail[c] = last.astype(jnp.bfloat16)
        x = jnp.concatenate([modes[c, 0:keep, :], tail[c]], 0)
        return lax.dot_general(x, x, NT, preferred_element_type=jnp.float32)

    total = gram_part(0)
    pl.semaphore_wait(barrier, wide + narrow - 2)

    copies = halo_copies(0)
    for copy in copies:
        copy.start()
    pending = list(copies)

    for c in range(1, comps):
        total = total + gram_part(c)
    gram[...] = total
    mine = pl.ds(pl.multiple_of(iw * piece_rows, piece_rows), piece_rows)
    scatter[iw] = gram[mine, :]
    first = []
    for d in range(1, wide):
        peer = w_peer(d)
        theirs = pl.ds(pl.multiple_of(peer * piece_rows, piece_rows), piece_rows)
        first.append(remote(gram.at[theirs], scatter.at[iw], red_send.at[0, d], red_recv.at[0, iw], (peer, jn)))
    for copy in first:
        copy.start()
    pending += first

    def reduce_step(s):
        started = []
        if s == 1:
            for d in range(1, wide):
                peer = w_peer(d)
                remote(gram.at[mine], scatter.at[peer], red_send.at[0, d], red_recv.at[0, peer], (peer, jn)).wait_recv()
            acc = scatter[0]
            for w in range(1, wide):
                acc = acc + scatter[w]
            part[...] = acc
            share[jn] = acc
            for d in range(1, narrow):
                started.append(remote(part, share.at[jn], red_send.at[1, d], red_recv.at[1, jn], (iw, n_peer(d))))
        elif s == 2:
            for d in range(1, narrow):
                peer = n_peer(d)
                remote(part, share.at[peer], red_send.at[1, d], red_recv.at[1, peer], (iw, peer)).wait_recv()
            acc = share[0]
            for n in range(1, narrow):
                acc = acc + share[n]
            piece[...] = acc
            whole[iw] = acc
            for d in range(1, wide):
                started.append(remote(piece, whole.at[iw], red_send.at[2, d], red_recv.at[2, iw], (w_peer(d), jn)))
        elif s == 3:
            for d in range(1, wide):
                peer = w_peer(d)
                remote(piece, whole.at[peer], red_send.at[2, d], red_recv.at[2, peer], (peer, jn)).wait_recv()
        for copy in started:
            copy.start()
        return started

    def send_snapshot(s):
        snap_in[s, jn] = packed[s + 1, (jn * z_own) // LANES]
        started = []
        for d in range(1, narrow):
            peer = n_peer(d)
            started.append(
                remote(packed.at[s + 1, (peer * z_own) // LANES], snap_in.at[s, jn],
                       snap_send.at[s, d], snap_recv.at[s, jn], (iw, peer))
            )
        for copy in started:
            copy.start()
        return started

    offset = lax.rem(jn * z_own, LANES)
    spread = (
        lax.rem(lax.broadcasted_iota(jnp.int32, (y_all, LANES), 1), y_all)
        == lax.broadcasted_iota(jnp.int32, (y_all, LANES), 0)
    ).astype(jnp.bfloat16)
    z_id = lax.broadcasted_iota(jnp.int32, (LANES, LANES), 0) - offset
    k_id = lax.broadcasted_iota(jnp.int32, (LANES, LANES), 1) // y_all
    fits = lax.rem(z_id + LANES, z_group) == k_id
    pick_row = lax.broadcasted_iota(jnp.int32, (16 * groups, LANES), 0)
    pick_z = lax.broadcasted_iota(jnp.int32, (16 * groups, LANES), 1) - offset
    inside = (pick_z >= 0) & (pick_z // z_group == pick_row // 16)

    def order_snapshot(s):
        for d in range(1, narrow):
            peer = n_peer(d)
            remote(packed.at[s + 1, 0], snap_in.at[s, peer], snap_send.at[s, d], snap_recv.at[s, peer], (iw, peer)).wait_recv()
        arrived = [snap_in[s, n].astype(jnp.float32) for n in range(narrow)]
        pick = (inside & (lax.rem(pick_row, 16) == 16 - stages + s)).astype(jnp.bfloat16)
        for c in range(comps):
            cells = jnp.concatenate([a[c * cells_y : (c + 1) * cells_y, :] for a in arrived], 0)
            wide_cells = lax.dot_general(
                cells.astype(jnp.bfloat16), spread, (((0,), (0,)), ((), ())), preferred_element_type=jnp.float32
            )
            chosen = jnp.where(fits, wide_cells, 0.0).astype(jnp.bfloat16)
            ordered = jnp.dot(pick, chosen, preferred_element_type=jnp.float32)
            flat = jnp.concatenate([ordered[16 * g : 16 * g + 16, :] for g in range(groups)], 1)
            tail[c] = (tail[c].astype(jnp.float32) + flat).astype(jnp.bfloat16)

    tiles, pivots = [], []
    inverse_cells = 1.0 / (wide * narrow * cells_y * cells_z)

    def begin():
        for t in range(columns // 8):
            rows = whole[(8 * t) // piece_rows, (8 * t) % piece_rows : (8 * t) % piece_rows + 8, :]
            tiles.append(rows * inverse_cells)

    def run(start, stop):
        for p in range(start, stop):
            pivots.append(eliminate_panel(tiles, p, 0, min(8, prior - 8 * p)))

    row = lax.broadcasted_iota(jnp.int32, (cells_y, cells_z), 0)
    base = current
    for s in range(stages):
        inner = inner_part(current)
        below = [pltpu.roll(c, 1, 0) for c in current]
        above = [pltpu.roll(c, cells_y - 1, 0) for c in current]
        for copy in copies:
            copy.wait_recv()
        x_low = unpack(x_halo.at[s, 0])
        x_high = unpack(x_halo.at[s, 1])
        y_low, y_high = [], []
        for c in range(comps):
            low = jnp.broadcast_to(y_halo[s, 0, c : c + 1, :], (cells_y, cells_z))
            high = jnp.broadcast_to(y_halo[s, 1, c : c + 1, :], (cells_y, cells_z))
            y_low.append(jnp.where(row == 0, low, below[c]))
            y_high.append(jnp.where(row == cells_y - 1, high, above[c]))
        change = [
            a + b + c for a, b, c in zip(inner, along(x_low, x_high, 0), along(y_low, y_high, 1))
        ]
        moved = [a + TIME_STEP * b for a, b in zip(current, change)]
        if s % 2 == 1:
            moved = [0.5 * a + 0.5 * b for a, b in zip(base, moved)]
            base = moved
        current = moved
        put_state(s + 1, current)
        if s + 1 < stages:
            copies = halo_copies(s + 1)
            for copy in copies:
                copy.start()
            pending += copies
        pending += send_snapshot(s)
        pending += reduce_step(s + 1)
        if s > 0:
            order_snapshot(s - 1)
        if s == stages - 2:
            begin()
            run(0, 4)
    for c in range(comps):
        flow[c] = current[c]

    run(4, 8)
    order_snapshot(stages - 1)
    total = jnp.zeros((columns, 16), jnp.float32)
    for c in range(comps):
        rows = tail[c]
        x = jnp.concatenate([modes[c, 0:keep, :], rows], 0)
        total = total + lax.dot_general(x, rows, NT, preferred_element_type=jnp.float32)
    mine8 = jnp.transpose(total)[8:16, :]
    rows8[...] = mine8
    rows_n[jn] = mine8
    started = [
        remote(rows8, rows_n.at[jn], last_send.at[0, d], last_recv.at[0, jn], (iw, n_peer(d)))
        for d in range(1, narrow)
    ]
    for copy in started:
        copy.start()
    pending += started
    run(8, 12)
    for d in range(1, narrow):
        peer = n_peer(d)
        remote(rows8, rows_n.at[peer], last_send.at[0, d], last_recv.at[0, peer], (iw, peer)).wait_recv()
    sum8 = rows_n[0]
    for n in range(1, narrow):
        sum8 = sum8 + rows_n[n]
    sums8[...] = sum8
    rows_w[iw] = sum8
    started = [
        remote(sums8, rows_w.at[iw], last_send.at[1, d], last_recv.at[1, iw], (w_peer(d), jn))
        for d in range(1, wide)
    ]
    for copy in started:
        copy.start()
    pending += started
    run(12, columns // 8)
    lane, row = lane_ids(), row_ids()
    uppers, inverse = [], []
    for t in range(columns // 8):
        scale = lax.rsqrt(jnp.where(pivots[t] > 0.0, pivots[t], 1.0))
        scale = jnp.where(row + 8 * t < prior, scale, 0.0)
        uppers.append(jnp.where(lane >= row + 8 * t, tiles[t], 0.0) * scale)
        left = jnp.where(lane < row + 8 * t, tiles[t], 0.0)
        inverse.append(jnp.where(lane == row + 8 * t, 1.0, left) * scale)
    inverse = jnp.concatenate(inverse, 0)
    for copy in pending:
        copy.wait_send()
    for d in range(1, wide):
        peer = w_peer(d)
        remote(sums8, rows_w.at[peer], last_send.at[1, d], last_recv.at[1, peer], (peer, jn)).wait_recv()
    sum8 = rows_w[0]
    for w in range(1, wide):
        sum8 = sum8 + rows_w[w]

    exact = lax.Precision.HIGHEST
    corner = row + columns - 8 >= prior
    rows = jnp.where(corner, sum8 * inverse_cells, 0.0)
    known = jnp.where(lane < prior, rows, 0.0)
    solved = lax.dot_general(known, inverse, NT, precision=exact, preferred_element_type=jnp.float32)
    bottom = jnp.concatenate([jnp.zeros((columns - 8, columns), jnp.float32), solved], 0)
    taken = lax.dot_general(solved, bottom, NT, precision=exact, preferred_element_type=jnp.float32)
    last_tile = [jnp.where(lane >= prior, rows - taken, 0.0)]
    last_tile = [pltpu.roll(last_tile[0], 8, 1)]
    left = eliminate_panel(last_tile, 0, prior - (columns - 8), 8)
    tip = jnp.where(lane >= row, last_tile[0], 0.0) * lax.rsqrt(jnp.where(corner, left, 1.0))
    tip = pltpu.roll(jnp.where(corner, tip, 0.0), LANES - 8, 1)
    side = jnp.transpose(bottom)
    for t in range(columns // 8):
        out = uppers[t] + side[8 * t : 8 * t + 8, :]
        if t == columns // 8 - 1:
            out = jnp.where(corner, tip, out)
        factor_out[8 * t : 8 * t + 8, :] = out


def local(wide, narrow, fields, prior_modes):
    comps, cells_x, cells_y, cells_z = fields.shape
    prior = prior_modes.shape[0]
    stages = 2 * STEPS
    columns = prior + stages
    modes = jnp.transpose(prior_modes, (1, 2, 0, 3)).reshape(comps, prior, prior_modes.shape[3])
    piece = columns // wide
    snap_rows = -(-comps * cells_y // 16) * 16
    f32, bf16 = jnp.float32, jnp.bfloat16
    vmem = pl.BlockSpec(memory_space=pltpu.VMEM)
    dma = pltpu.SemaphoreType.DMA
    flow, factor = pl.pallas_call(
        functools.partial(kernel, wide, narrow),
        out_shape=(
            jax.ShapeDtypeStruct((comps, cells_y, cells_z), f32),
            jax.ShapeDtypeStruct((columns, columns), f32),
        ),
        in_specs=[pl.BlockSpec(memory_space=pltpu.HBM)] * 2,
        out_specs=(vmem, vmem),
        scratch_shapes=[
            pltpu.VMEM(modes.shape, bf16), dma((comps,)),
            pltpu.VMEM((comps, cells_y, cells_z), f32), dma((1,)),
            pltpu.VMEM((stages + 1, cells_z // LANES, snap_rows, LANES), bf16),
            pltpu.VMEM((stages, 2, cells_z // LANES, snap_rows, LANES), bf16),
            pltpu.VMEM((stages, 2, 8, cells_z), f32),
            pltpu.VMEM((stages, 2, 8, cells_z), f32),
            dma((stages, 4)), dma((stages, 4)),
            pltpu.VMEM((stages, narrow, snap_rows, LANES), bf16),
            dma((stages, narrow)), dma((stages, narrow)),
            pltpu.VMEM((columns, columns), f32),
            pltpu.VMEM((wide, piece, columns), f32),
            pltpu.VMEM((piece, columns), f32),
            pltpu.VMEM((narrow, piece, columns), f32),
            pltpu.VMEM((wide, piece, columns), f32),
            pltpu.VMEM((piece, columns), f32),
            dma((3, max(wide, narrow))), dma((3, max(wide, narrow))),
            pltpu.VMEM((comps, 16, modes.shape[2]), bf16),
            pltpu.VMEM((8, columns), f32),
            pltpu.VMEM((narrow, 8, columns), f32),
            pltpu.VMEM((8, columns), f32),
            pltpu.VMEM((wide, 8, columns), f32),
            dma((2, max(wide, narrow))), dma((2, max(wide, narrow))),
        ],
        compiler_params=pltpu.CompilerParams(
            collective_id=0, has_side_effects=True, vmem_limit_bytes=52 * 1024 * 1024
        ),
    )(fields.reshape(comps, cells_y, cells_z), modes)
    return flow.reshape(fields.shape), factor


def solution(mesh):
    wide, narrow = mesh.shape["wide"], mesh.shape["narrow"]
    return jax.shard_map(
        functools.partial(local, wide, narrow),
        mesh=mesh,
        in_specs=(P(None, "wide", "narrow", None), P(None, None, "wide", "narrow")),
        out_specs=(P(None, "wide", "narrow", None), P()),
        check_vma=False,
    )
```

```python
import functools

import jax
import jax.numpy as jnp
from jax import lax
from jax.experimental import pallas as pl
from jax.experimental.pallas import tpu as pltpu
from jax.sharding import PartitionSpec as P

STEPS = 2
GAMMA = 1.4
TIME_STEP = 0.25
VISCOSITY = 0.15
LANES = 128
NT = (((1,), (1,)), ((), ()))


def flux_of(state, d):
    density, energy = state[0], state[4]
    momentum = state[1:4]
    inverse = 1.0 / density
    vel = momentum[d] * inverse
    squares = momentum[0] * momentum[0] + momentum[1] * momentum[1] + momentum[2] * momentum[2]
    pressure = (GAMMA - 1.0) * (energy - 0.5 * squares * inverse)
    out = [momentum[d], momentum[0] * vel, momentum[1] * vel, momentum[2] * vel]
    out.append((energy + pressure) * vel)
    out[1 + d] = out[1 + d] + pressure
    return out


def along(low, high, d):
    return [
        -0.5 * (fh - fl) + VISCOSITY * (l + h)
        for fh, fl, l, h in zip(flux_of(high, d), flux_of(low, d), low, high)
    ]


def inner_part(here):
    cells_z = here[0].shape[1]
    z_low = [pltpu.roll(c, 1, 1) for c in here]
    z_high = [pltpu.roll(c, cells_z - 1, 1) for c in here]
    return [a - (6.0 * VISCOSITY) * c for a, c in zip(along(z_low, z_high, 2), here)]


def lane_ids():
    return lax.broadcasted_iota(jnp.int32, (8, LANES), 1)


def row_ids():
    return lax.broadcasted_iota(jnp.int32, (8, LANES), 0)


def column_of(tile, j):
    return jnp.broadcast_to(tile[:, j : j + 1], (8, LANES))


def row_of(tile, k):
    return jnp.broadcast_to(tile[k : k + 1, :], (8, LANES))


def inverted(x):
    guess = pl.reciprocal(x, approx=True)
    guess = guess * (2.0 - x * guess)
    return guess * (2.0 - x * guess)


def eliminate_panel(tiles, p, first, last):
    lane, row = lane_ids(), row_ids()
    steps = range(first, last)
    panel = tiles[p]
    inside = (lane >= 8 * p + first) & (lane < 8 * p + last)
    spread = {k: column_of(panel, 8 * p + k) for k in steps}
    entry = {(m, k): row_of(spread[k], m) for k in steps for m in range(k, last)}
    inverses, ratio = {}, {}
    for k in steps:
        inverses[k] = inverted(entry[k, k])
        for m in range(k + 1, last):
            ratio[m, k] = entry[m, k] * inverses[k]
            for n in range(m, last):
                entry[n, m] = entry[n, m] - entry[n, k] * ratio[m, k]
    raw = {k: row_of(panel, k) for k in steps}
    heads = {k: jnp.where(inside, jnp.where(lane == 8 * p + k, 1.0, 0.0), raw[k]) for k in steps}
    for k in steps:
        for m in range(first, k):
            raw[k] = raw[k] - ratio[k, m] * raw[m]
            heads[k] = heads[k] - ratio[k, m] * heads[m]
    pivots = jnp.zeros((8, LANES), jnp.float32)
    panel = jnp.zeros((8, LANES), jnp.float32)
    for k in steps:
        pivots = jnp.where(row == k, entry[k, k], pivots)
        panel = jnp.where(row == k, jnp.where(inside & (lane < 8 * p + k), heads[k], raw[k]), panel)
    tiles[p] = panel
    for t in range(p + 1, len(tiles)):
        rest = jnp.where(inside, 0.0, tiles[t])
        factors = {}
        for k in steps:
            left = column_of(tiles[t], 8 * p + k)
            for m in range(first, k):
                left = left - factors[m] * entry[k, m]
            factors[k] = left * inverses[k]
            rest = rest - factors[k] * heads[k]
        tiles[t] = rest
    return pivots


def kernel(
    wide, narrow, fields, modes_hbm, flow, factor_out,
    modes, modes_sem, start, start_sem, packed, x_halo, y_send, y_halo, d_halo, halo_send, halo_recv,
    snap_in, snap_send, snap_recv,
    gram, scatter, part, share, whole, piece, red_send, red_recv,
    tail, rows8, rows_n, sums8, rows_w, last_send, last_recv,
):
    stages = 2 * STEPS
    comps, cells_y, cells_z = fields.shape
    prior = modes.shape[1]
    columns = gram.shape[0]
    mode_lanes = modes.shape[2]
    y_all = cells_y * narrow
    z_own = cells_z // narrow
    z_group = LANES // y_all
    groups = mode_lanes // LANES
    piece_rows = columns // wide
    keep = columns - 16
    iw, jn = lax.axis_index("wide"), lax.axis_index("narrow")

    w_peers = [lax.rem(iw + d, wide) for d in range(wide)]
    n_peers = [lax.rem(jn + d, narrow) for d in range(narrow)]

    def w_peer(d):
        return w_peers[d % wide]

    def n_peer(d):
        return n_peers[d % narrow]

    def remote(src, dst, send, recv, device):
        return pltpu.make_async_remote_copy(
            src_ref=src, dst_ref=dst, send_sem=send, recv_sem=recv,
            device_id=device, device_id_type=pl.DeviceIdType.MESH,
        )

    loads = [pltpu.make_async_copy(modes_hbm.at[c], modes.at[c], modes_sem.at[c]) for c in range(comps)]
    fields_load = pltpu.make_async_copy(fields, start, start_sem.at[0])
    fields_load.start()
    for load in loads:
        load.start()

    barrier = pltpu.get_barrier_semaphore()
    for d in range(1, wide):
        pl.semaphore_signal(barrier, inc=1, device_id=(w_peer(d), jn), device_id_type=pl.DeviceIdType.MESH)
    for d in range(1, narrow):
        pl.semaphore_signal(barrier, inc=1, device_id=(iw, n_peer(d)), device_id_type=pl.DeviceIdType.MESH)

    for d in (1, wide - 1):
        for e in (1, narrow - 1):
            pl.semaphore_signal(barrier, inc=1, device_id=(w_peer(d), n_peer(e)), device_id_type=pl.DeviceIdType.MESH)

    def halo_copies(q):
        moves = []
        for side, d in enumerate((1, -1, 2, -2)):
            moves.append((packed.at[2 * q], x_halo.at[q, side], (w_peer(d), jn)))
        for e, y_side in ((1, 0), (-1, 1)):
            moves.append((y_send.at[q, 1 - y_side], y_halo.at[q, y_side], (iw, n_peer(e))))
            for d, x_side in ((1, 0), (-1, 1)):
                moves.append((y_send.at[q, 1 - y_side, 0], d_halo.at[q, x_side, y_side], (w_peer(d), n_peer(e))))
        return [
            remote(src, dst, halo_send.at[q, i], halo_recv.at[q, i], device)
            for i, (src, dst, device) in enumerate(moves)
        ]

    def put_state(s, values):
        spare = jnp.zeros((packed.shape[2] - comps * cells_y, cells_z), jnp.float32)
        stacked = jnp.concatenate(values + [spare], 0).astype(jnp.bfloat16)
        for b in range(cells_z // LANES):
            packed[s, b] = stacked[:, b * LANES : (b + 1) * LANES]
        if s % 2 == 0 and s < stages:
            for depth in range(2):
                for c in range(comps):
                    y_send[s // 2, 0, depth, c : c + 1, :] = values[c][depth : depth + 1, :]
                    top = cells_y - 1 - depth
                    y_send[s // 2, 1, depth, c : c + 1, :] = values[c][top : top + 1, :]
                for c in range(comps, 8):
                    y_send[s // 2, 0, depth, c : c + 1, :] = jnp.zeros((1, cells_z), jnp.float32)
                    y_send[s // 2, 1, depth, c : c + 1, :] = jnp.zeros((1, cells_z), jnp.float32)

    def unpack(ref):
        blocks = [ref[b].astype(jnp.float32) for b in range(cells_z // LANES)]
        return [
            jnp.concatenate([x[c * cells_y : (c + 1) * cells_y, :] for x in blocks], 1)
            for c in range(comps)
        ]

    fields_load.wait()
    current = [start[c] for c in range(comps)]
    put_state(0, current)
    def gram_part(c):
        loads[c].wait()
        last = modes[c, keep:prior, :].astype(jnp.float32)
        last = jnp.concatenate([last, jnp.zeros((columns - prior, mode_lanes), jnp.float32)], 0)
        tail[c] = last.astype(jnp.bfloat16)
        x = jnp.concatenate([modes[c, 0:keep, :], tail[c]], 0)
        return lax.dot_general(x, x, NT, preferred_element_type=jnp.float32)

    total = gram_part(0)
    pl.semaphore_wait(barrier, wide + narrow + 2)

    copies = halo_copies(0)
    for copy in copies:
        copy.start()
    pending = list(copies)

    for c in range(1, comps):
        total = total + gram_part(c)
    gram[...] = total
    mine = pl.ds(pl.multiple_of(iw * piece_rows, piece_rows), piece_rows)
    scatter[iw] = gram[mine, :]
    first = []
    for d in range(1, wide):
        peer = w_peer(d)
        theirs = pl.ds(pl.multiple_of(peer * piece_rows, piece_rows), piece_rows)
        first.append(remote(gram.at[theirs], scatter.at[iw], red_send.at[0, d], red_recv.at[0, iw], (peer, jn)))
    for copy in first:
        copy.start()
    pending += first

    def reduce_step(s):
        started = []
        if s == 1:
            for d in range(1, wide):
                peer = w_peer(d)
                remote(gram.at[mine], scatter.at[peer], red_send.at[0, d], red_recv.at[0, peer], (peer, jn)).wait_recv()
            acc = scatter[0]
            for w in range(1, wide):
                acc = acc + scatter[w]
            part[...] = acc
            share[jn] = acc
            for d in range(1, narrow):
                started.append(remote(part, share.at[jn], red_send.at[1, d], red_recv.at[1, jn], (iw, n_peer(d))))
        elif s == 2:
            for d in range(1, narrow):
                peer = n_peer(d)
                remote(part, share.at[peer], red_send.at[1, d], red_recv.at[1, peer], (iw, peer)).wait_recv()
            acc = share[0]
            for n in range(1, narrow):
                acc = acc + share[n]
            piece[...] = acc
            whole[iw] = acc
            for d in range(1, wide):
                started.append(remote(piece, whole.at[iw], red_send.at[2, d], red_recv.at[2, iw], (w_peer(d), jn)))
        elif s == 3:
            for d in range(1, wide):
                peer = w_peer(d)
                remote(piece, whole.at[peer], red_send.at[2, d], red_recv.at[2, peer], (peer, jn)).wait_recv()
        for copy in started:
            copy.start()
        return started

    def send_snapshot(s):
        snap_in[s, jn] = packed[s + 1, (jn * z_own) // LANES]
        started = []
        for d in range(1, narrow):
            peer = n_peer(d)
            started.append(
                remote(packed.at[s + 1, (peer * z_own) // LANES], snap_in.at[s, jn],
                       snap_send.at[s, d], snap_recv.at[s, jn], (iw, peer))
            )
        for copy in started:
            copy.start()
        return started

    offset = lax.rem(jn * z_own, LANES)
    spread = (
        lax.rem(lax.broadcasted_iota(jnp.int32, (y_all, LANES), 1), y_all)
        == lax.broadcasted_iota(jnp.int32, (y_all, LANES), 0)
    ).astype(jnp.bfloat16)
    z_id = lax.broadcasted_iota(jnp.int32, (LANES, LANES), 0) - offset
    k_id = lax.broadcasted_iota(jnp.int32, (LANES, LANES), 1) // y_all
    fits = lax.rem(z_id + LANES, z_group) == k_id
    pick_row = lax.broadcasted_iota(jnp.int32, (16 * groups, LANES), 0)
    pick_z = lax.broadcasted_iota(jnp.int32, (16 * groups, LANES), 1) - offset
    inside = (pick_z >= 0) & (pick_z // z_group == pick_row // 16)

    def order_snapshot(s):
        for d in range(1, narrow):
            peer = n_peer(d)
            remote(packed.at[s + 1, 0], snap_in.at[s, peer], snap_send.at[s, d], snap_recv.at[s, peer], (iw, peer)).wait_recv()
        arrived = [snap_in[s, n].astype(jnp.float32) for n in range(narrow)]
        pick = (inside & (lax.rem(pick_row, 16) == 16 - stages + s)).astype(jnp.bfloat16)
        for c in range(comps):
            cells = jnp.concatenate([a[c * cells_y : (c + 1) * cells_y, :] for a in arrived], 0)
            wide_cells = lax.dot_general(
                cells.astype(jnp.bfloat16), spread, (((0,), (0,)), ((), ())), preferred_element_type=jnp.float32
            )
            chosen = jnp.where(fits, wide_cells, 0.0).astype(jnp.bfloat16)
            ordered = jnp.dot(pick, chosen, preferred_element_type=jnp.float32)
            flat = jnp.concatenate([ordered[16 * g : 16 * g + 16, :] for g in range(groups)], 1)
            tail[c] = (tail[c].astype(jnp.float32) + flat).astype(jnp.bfloat16)

    tiles, pivots = [], []
    inverse_cells = 1.0 / (wide * narrow * cells_y * cells_z)

    def begin():
        for t in range(columns // 8):
            rows = whole[(8 * t) // piece_rows, (8 * t) % piece_rows : (8 * t) % piece_rows + 8, :]
            tiles.append(rows * inverse_cells)

    def run(start, stop):
        for p in range(start, stop):
            pivots.append(eliminate_panel(tiles, p, 0, min(8, prior - 8 * p)))

    row = lax.broadcasted_iota(jnp.int32, (cells_y, cells_z), 0)

    def line(values, k):
        return [jnp.broadcast_to(v[k : k + 1, :], (cells_y, cells_z)) for v in values]

    def lines(ref):
        return [jnp.broadcast_to(ref[c : c + 1, :], (cells_y, cells_z)) for c in range(comps)]

    def either(low, high):
        return [jnp.where(row == 0, a, b) for a, b in zip(low, high)]

    def shifted(here, low, high):
        below = [jnp.where(row == 0, a, pltpu.roll(c, 1, 0)) for a, c in zip(low, here)]
        above = [
            jnp.where(row == cells_y - 1, a, pltpu.roll(c, cells_y - 1, 0)) for a, c in zip(high, here)
        ]
        return below, above

    def change_of(inner, x_low, x_high, y_low, y_high):
        return [a + b + c for a, b, c in zip(inner, along(x_low, x_high, 0), along(y_low, y_high, 1))]

    def moved(here, inner, x_low, x_high, y_low, y_high):
        change = change_of(inner, x_low, x_high, y_low, y_high)
        return [a + TIME_STEP * b for a, b in zip(here, change)]

    for q in range(STEPS):
        inner = inner_part(current)
        for copy in copies:
            copy.wait_recv()
        planes = [unpack(x_halo.at[q, side]) for side in range(4)]
        low, high = lines(y_halo.at[q, 0, 0]), lines(y_halo.at[q, 1, 0])
        corner = [[lines(d_halo.at[q, i, j]) for j in range(2)] for i in range(2)]
        first_own = moved(current, inner, planes[0], planes[1], *shifted(current, low, high))
        put_state(2 * q + 1, first_own)
        pending += send_snapshot(2 * q)
        first_low = moved(
            planes[0], inner_part(planes[0]), planes[2], current, *shifted(planes[0], *corner[0])
        )
        first_high = moved(
            planes[1], inner_part(planes[1]), current, planes[3], *shifted(planes[1], *corner[1])
        )
        rim = either(low, high)
        first_rim = moved(
            rim, inner_part(rim), either(*corner[0]), either(*corner[1]),
            either(lines(y_halo.at[q, 0, 1]), line(current, cells_y - 1)),
            either(line(current, 0), lines(y_halo.at[q, 1, 1])),
        )
        second = moved(
            first_own, inner_part(first_own), first_low, first_high,
            *shifted(first_own, line(first_rim, 0), line(first_rim, 1)),
        )
        current = [0.5 * a + 0.5 * b for a, b in zip(current, second)]
        put_state(2 * q + 2, current)
        if q + 1 < STEPS:
            copies = halo_copies(q + 1)
            for copy in copies:
                copy.start()
            pending += copies
        pending += send_snapshot(2 * q + 1)
        if q == 0:
            pending += reduce_step(1)
            order_snapshot(0)
            pending += reduce_step(2)
    reduce_step(3)
    begin()
    run(0, 3)
    for s in range(1, stages - 1):
        order_snapshot(s)
    for c in range(comps):
        flow[c] = current[c]

    order_snapshot(stages - 1)
    total = jnp.zeros((columns, 16), jnp.float32)
    for c in range(comps):
        rows = tail[c]
        x = jnp.concatenate([modes[c, 0:keep, :], rows], 0)
        total = total + lax.dot_general(x, rows, NT, preferred_element_type=jnp.float32)
    mine8 = jnp.transpose(total)[8:16, :]
    rows8[...] = mine8
    rows_n[jn] = mine8
    started = [
        remote(rows8, rows_n.at[jn], last_send.at[0, d], last_recv.at[0, jn], (iw, n_peer(d)))
        for d in range(1, narrow)
    ]
    for copy in started:
        copy.start()
    pending += started
    run(3, 9)
    for d in range(1, narrow):
        peer = n_peer(d)
        remote(rows8, rows_n.at[peer], last_send.at[0, d], last_recv.at[0, peer], (iw, peer)).wait_recv()
    sum8 = rows_n[0]
    for n in range(1, narrow):
        sum8 = sum8 + rows_n[n]
    sums8[...] = sum8
    rows_w[iw] = sum8
    started = [
        remote(sums8, rows_w.at[iw], last_send.at[1, d], last_recv.at[1, iw], (w_peer(d), jn))
        for d in range(1, wide)
    ]
    for copy in started:
        copy.start()
    pending += started
    run(9, columns // 8)
    lane, row = lane_ids(), row_ids()
    uppers, inverse = [], []
    for t in range(columns // 8):
        scale = lax.rsqrt(jnp.where(pivots[t] > 0.0, pivots[t], 1.0))
        scale = jnp.where(row + 8 * t < prior, scale, 0.0)
        uppers.append(jnp.where(lane >= row + 8 * t, tiles[t], 0.0) * scale)
        left = jnp.where(lane < row + 8 * t, tiles[t], 0.0)
        inverse.append(jnp.where(lane == row + 8 * t, 1.0, left) * scale)
    inverse = jnp.concatenate(inverse, 0)
    for copy in pending:
        copy.wait_send()
    for d in range(1, wide):
        peer = w_peer(d)
        remote(sums8, rows_w.at[peer], last_send.at[1, d], last_recv.at[1, peer], (peer, jn)).wait_recv()
    sum8 = rows_w[0]
    for w in range(1, wide):
        sum8 = sum8 + rows_w[w]

    exact = lax.Precision.HIGHEST
    corner = row + columns - 8 >= prior
    rows = jnp.where(corner, sum8 * inverse_cells, 0.0)
    known = jnp.where(lane < prior, rows, 0.0)
    solved = lax.dot_general(known, inverse, NT, precision=exact, preferred_element_type=jnp.float32)
    bottom = jnp.concatenate([jnp.zeros((columns - 8, columns), jnp.float32), solved], 0)
    taken = lax.dot_general(solved, bottom, NT, precision=exact, preferred_element_type=jnp.float32)
    last_tile = [jnp.where(lane >= prior, rows - taken, 0.0)]
    last_tile = [pltpu.roll(last_tile[0], 8, 1)]
    left = eliminate_panel(last_tile, 0, prior - (columns - 8), 8)
    tip = jnp.where(lane >= row, last_tile[0], 0.0) * lax.rsqrt(jnp.where(corner, left, 1.0))
    tip = pltpu.roll(jnp.where(corner, tip, 0.0), LANES - 8, 1)
    side = jnp.transpose(bottom)
    for t in range(columns // 8):
        out = uppers[t] + side[8 * t : 8 * t + 8, :]
        if t == columns // 8 - 1:
            out = jnp.where(corner, tip, out)
        factor_out[8 * t : 8 * t + 8, :] = out


def local(wide, narrow, fields, prior_modes):
    comps, cells_x, cells_y, cells_z = fields.shape
    prior = prior_modes.shape[0]
    stages = 2 * STEPS
    columns = prior + stages
    modes = jnp.transpose(prior_modes, (1, 2, 0, 3)).reshape(comps, prior, prior_modes.shape[3])
    piece = columns // wide
    snap_rows = -(-comps * cells_y // 16) * 16
    f32, bf16 = jnp.float32, jnp.bfloat16
    vmem = pl.BlockSpec(memory_space=pltpu.VMEM)
    dma = pltpu.SemaphoreType.DMA
    flow, factor = pl.pallas_call(
        functools.partial(kernel, wide, narrow),
        out_shape=(
            jax.ShapeDtypeStruct((comps, cells_y, cells_z), f32),
            jax.ShapeDtypeStruct((columns, columns), f32),
        ),
        in_specs=[pl.BlockSpec(memory_space=pltpu.HBM)] * 2,
        out_specs=(vmem, vmem),
        scratch_shapes=[
            pltpu.VMEM(modes.shape, bf16), dma((comps,)),
            pltpu.VMEM((comps, cells_y, cells_z), f32), dma((1,)),
            pltpu.VMEM((stages + 1, cells_z // LANES, snap_rows, LANES), bf16),
            pltpu.VMEM((STEPS, 4, cells_z // LANES, snap_rows, LANES), bf16),
            pltpu.VMEM((STEPS, 2, 2, 8, cells_z), f32),
            pltpu.VMEM((STEPS, 2, 2, 8, cells_z), f32),
            pltpu.VMEM((STEPS, 2, 2, 8, cells_z), f32),
            dma((STEPS, 10)), dma((STEPS, 10)),
            pltpu.VMEM((stages, narrow, snap_rows, LANES), bf16),
            dma((stages, narrow)), dma((stages, narrow)),
            pltpu.VMEM((columns, columns), f32),
            pltpu.VMEM((wide, piece, columns), f32),
            pltpu.VMEM((piece, columns), f32),
            pltpu.VMEM((narrow, piece, columns), f32),
            pltpu.VMEM((wide, piece, columns), f32),
            pltpu.VMEM((piece, columns), f32),
            dma((3, max(wide, narrow))), dma((3, max(wide, narrow))),
            pltpu.VMEM((comps, 16, modes.shape[2]), bf16),
            pltpu.VMEM((8, columns), f32),
            pltpu.VMEM((narrow, 8, columns), f32),
            pltpu.VMEM((8, columns), f32),
            pltpu.VMEM((wide, 8, columns), f32),
            dma((2, max(wide, narrow))), dma((2, max(wide, narrow))),
        ],
        compiler_params=pltpu.CompilerParams(
            collective_id=0, has_side_effects=True, vmem_limit_bytes=52 * 1024 * 1024
        ),
    )(fields.reshape(comps, cells_y, cells_z), modes)
    return flow.reshape(fields.shape), factor


def solution(mesh):
    wide, narrow = mesh.shape["wide"], mesh.shape["narrow"]
    return jax.shard_map(
        functools.partial(local, wide, narrow),
        mesh=mesh,
        in_specs=(P(None, "wide", "narrow", None), P(None, None, "wide", "narrow")),
        out_specs=(P(None, "wide", "narrow", None), P()),
        check_vma=False,
    )
```

```python
import functools

import jax
import jax.numpy as jnp
from jax import lax
from jax.experimental import pallas as pl
from jax.experimental.pallas import tpu as pltpu
from jax.sharding import PartitionSpec as P

STEPS = 2
GAMMA = 1.4
TIME_STEP = 0.25
VISCOSITY = 0.15
LANES = 128
NT = (((1,), (1,)), ((), ()))


def flux_of(state, d):
    density, energy = state[0], state[4]
    momentum = state[1:4]
    inverse = 1.0 / density
    vel = momentum[d] * inverse
    squares = momentum[0] * momentum[0] + momentum[1] * momentum[1] + momentum[2] * momentum[2]
    pressure = (GAMMA - 1.0) * (energy - 0.5 * squares * inverse)
    out = [momentum[d], momentum[0] * vel, momentum[1] * vel, momentum[2] * vel]
    out.append((energy + pressure) * vel)
    out[1 + d] = out[1 + d] + pressure
    return out


def along(low, high, d):
    return [
        -0.5 * (fh - fl) + VISCOSITY * (l + h)
        for fh, fl, l, h in zip(flux_of(high, d), flux_of(low, d), low, high)
    ]


def inner_part(here):
    cells_z = here[0].shape[1]
    z_low = [pltpu.roll(c, 1, 1) for c in here]
    z_high = [pltpu.roll(c, cells_z - 1, 1) for c in here]
    return [a - (6.0 * VISCOSITY) * c for a, c in zip(along(z_low, z_high, 2), here)]


def lane_ids():
    return lax.broadcasted_iota(jnp.int32, (8, LANES), 1)


def row_ids():
    return lax.broadcasted_iota(jnp.int32, (8, LANES), 0)


def column_of(tile, j):
    return jnp.broadcast_to(tile[:, j : j + 1], (8, LANES))


def row_of(tile, k):
    return jnp.broadcast_to(tile[k : k + 1, :], (8, LANES))


def inverted(x):
    guess = pl.reciprocal(x, approx=True)
    guess = guess * (2.0 - x * guess)
    return guess * (2.0 - x * guess)


def eliminate_panel(tiles, p, first, last):
    lane, row = lane_ids(), row_ids()
    steps = range(first, last)
    panel = tiles[p]
    inside = (lane >= 8 * p + first) & (lane < 8 * p + last)
    spread = {k: column_of(panel, 8 * p + k) for k in steps}
    entry = {(m, k): row_of(spread[k], m) for k in steps for m in range(k, last)}
    inverses, ratio = {}, {}
    for k in steps:
        inverses[k] = inverted(entry[k, k])
        for m in range(k + 1, last):
            ratio[m, k] = entry[m, k] * inverses[k]
            for n in range(m, last):
                entry[n, m] = entry[n, m] - entry[n, k] * ratio[m, k]
    raw = {k: row_of(panel, k) for k in steps}
    heads = {k: jnp.where(inside, jnp.where(lane == 8 * p + k, 1.0, 0.0), raw[k]) for k in steps}
    for k in steps:
        for m in range(first, k):
            raw[k] = raw[k] - ratio[k, m] * raw[m]
            heads[k] = heads[k] - ratio[k, m] * heads[m]
    pivots = jnp.zeros((8, LANES), jnp.float32)
    panel = jnp.zeros((8, LANES), jnp.float32)
    for k in steps:
        pivots = jnp.where(row == k, entry[k, k], pivots)
        panel = jnp.where(row == k, jnp.where(inside & (lane < 8 * p + k), heads[k], raw[k]), panel)
    tiles[p] = panel
    for t in range(p + 1, len(tiles)):
        rest = jnp.where(inside, 0.0, tiles[t])
        factors = {}
        for k in steps:
            left = column_of(tiles[t], 8 * p + k)
            for m in range(first, k):
                left = left - factors[m] * entry[k, m]
            factors[k] = left * inverses[k]
            rest = rest - factors[k] * heads[k]
        tiles[t] = rest
    return pivots


def kernel(
    wide, narrow, fields, modes_hbm, flow, factor_out,
    modes, modes_sem, start, start_sem, packed, x_halo, y_send, y_halo, d_halo, halo_send, halo_recv,
    snap_in, snap_send, snap_recv,
    gram, scatter, part, share, whole, piece, red_send, red_recv,
    tail, rows8, rows_n, sums8, rows_w, last_send, last_recv,
):
    stages = 2 * STEPS
    comps, cells_y, cells_z = fields.shape
    prior = modes.shape[1]
    columns = gram.shape[0]
    mode_lanes = modes.shape[2]
    y_all = cells_y * narrow
    z_own = cells_z // narrow
    z_group = LANES // y_all
    groups = mode_lanes // LANES
    piece_rows = columns // wide
    keep = columns - 16
    iw, jn = lax.axis_index("wide"), lax.axis_index("narrow")

    w_peers = [lax.rem(iw + d, wide) for d in range(wide)]
    n_peers = [lax.rem(jn + d, narrow) for d in range(narrow)]

    def w_peer(d):
        return w_peers[d % wide]

    def n_peer(d):
        return n_peers[d % narrow]

    def remote(src, dst, send, recv, device):
        return pltpu.make_async_remote_copy(
            src_ref=src, dst_ref=dst, send_sem=send, recv_sem=recv,
            device_id=device, device_id_type=pl.DeviceIdType.MESH,
        )

    loads = [pltpu.make_async_copy(modes_hbm.at[c], modes.at[c], modes_sem.at[c]) for c in range(comps)]
    fields_load = pltpu.make_async_copy(fields, start, start_sem.at[0])
    fields_load.start()
    for load in loads:
        load.start()

    barrier = pltpu.get_barrier_semaphore()
    for d in range(1, wide):
        pl.semaphore_signal(barrier, inc=1, device_id=(w_peer(d), jn), device_id_type=pl.DeviceIdType.MESH)
    for d in range(1, narrow):
        pl.semaphore_signal(barrier, inc=1, device_id=(iw, n_peer(d)), device_id_type=pl.DeviceIdType.MESH)

    for d in (1, wide - 1):
        for e in (1, narrow - 1):
            pl.semaphore_signal(barrier, inc=1, device_id=(w_peer(d), n_peer(e)), device_id_type=pl.DeviceIdType.MESH)

    def halo_copies(q):
        moves = []
        for side, d in enumerate((1, -1, 2, -2)):
            moves.append((packed.at[2 * q], x_halo.at[q, side], (w_peer(d), jn)))
        for e, y_side in ((1, 0), (-1, 1)):
            moves.append((y_send.at[q, 1 - y_side], y_halo.at[q, y_side], (iw, n_peer(e))))
            for d, x_side in ((1, 0), (-1, 1)):
                moves.append((y_send.at[q, 1 - y_side, 0], d_halo.at[q, x_side, y_side], (w_peer(d), n_peer(e))))
        return [
            remote(src, dst, halo_send.at[q, i], halo_recv.at[q, i], device)
            for i, (src, dst, device) in enumerate(moves)
        ]

    def put_state(s, values):
        spare = jnp.zeros((packed.shape[2] - comps * cells_y, cells_z), jnp.float32)
        stacked = jnp.concatenate(values + [spare], 0).astype(jnp.bfloat16)
        for b in range(cells_z // LANES):
            packed[s, b] = stacked[:, b * LANES : (b + 1) * LANES]
        if s % 2 == 0 and s < stages:
            for depth in range(2):
                for c in range(comps):
                    y_send[s // 2, 0, depth, c : c + 1, :] = values[c][depth : depth + 1, :]
                    top = cells_y - 1 - depth
                    y_send[s // 2, 1, depth, c : c + 1, :] = values[c][top : top + 1, :]
                for c in range(comps, 8):
                    y_send[s // 2, 0, depth, c : c + 1, :] = jnp.zeros((1, cells_z), jnp.float32)
                    y_send[s // 2, 1, depth, c : c + 1, :] = jnp.zeros((1, cells_z), jnp.float32)

    def unpack(ref):
        blocks = [ref[b].astype(jnp.float32) for b in range(cells_z // LANES)]
        return [
            jnp.concatenate([x[c * cells_y : (c + 1) * cells_y, :] for x in blocks], 1)
            for c in range(comps)
        ]

    fields_load.wait()
    current = [start[c] for c in range(comps)]
    put_state(0, current)
    def gram_part(c):
        loads[c].wait()
        last = modes[c, keep:prior, :].astype(jnp.float32)
        last = jnp.concatenate([last, jnp.zeros((columns - prior, mode_lanes), jnp.float32)], 0)
        tail[c] = last.astype(jnp.bfloat16)
        x = jnp.concatenate([modes[c, 0:keep, :], tail[c]], 0)
        return lax.dot_general(x, x, NT, preferred_element_type=jnp.float32)

    total = gram_part(0)
    pl.semaphore_wait(barrier, wide + narrow + 2)

    copies = halo_copies(0)
    for copy in copies:
        copy.start()
    pending = list(copies)

    for c in range(1, comps):
        total = total + gram_part(c)
    gram[...] = total
    mine = pl.ds(pl.multiple_of(iw * piece_rows, piece_rows), piece_rows)
    scatter[iw] = gram[mine, :]
    first = []
    for d in range(1, wide):
        peer = w_peer(d)
        theirs = pl.ds(pl.multiple_of(peer * piece_rows, piece_rows), piece_rows)
        first.append(remote(gram.at[theirs], scatter.at[iw], red_send.at[0, d], red_recv.at[0, iw], (peer, jn)))
    for copy in first:
        copy.start()
    pending += first

    def reduce_step(s):
        started = []
        if s == 1:
            for d in range(1, wide):
                peer = w_peer(d)
                remote(gram.at[mine], scatter.at[peer], red_send.at[0, d], red_recv.at[0, peer], (peer, jn)).wait_recv()
            acc = scatter[0]
            for w in range(1, wide):
                acc = acc + scatter[w]
            part[...] = acc
            share[jn] = acc
            for d in range(1, narrow):
                started.append(remote(part, share.at[jn], red_send.at[1, d], red_recv.at[1, jn], (iw, n_peer(d))))
        elif s == 2:
            for d in range(1, narrow):
                peer = n_peer(d)
                remote(part, share.at[peer], red_send.at[1, d], red_recv.at[1, peer], (iw, peer)).wait_recv()
            acc = share[0]
            for n in range(1, narrow):
                acc = acc + share[n]
            piece[...] = acc
            whole[iw] = acc
            for d in range(1, wide):
                started.append(remote(piece, whole.at[iw], red_send.at[2, d], red_recv.at[2, iw], (w_peer(d), jn)))
        elif s == 3:
            for d in range(1, wide):
                peer = w_peer(d)
                remote(piece, whole.at[peer], red_send.at[2, d], red_recv.at[2, peer], (peer, jn)).wait_recv()
        for copy in started:
            copy.start()
        return started

    def send_snapshots(q):
        own, made = pl.ds(2 * q, 2), pl.ds(2 * q + 1, 2)
        for i in range(2):
            snap_in[2 * q + i, jn] = packed[2 * q + 1 + i, (jn * z_own) // LANES]
        started = []
        for d in range(1, narrow):
            peer = n_peer(d)
            started.append(
                remote(packed.at[made, (peer * z_own) // LANES], snap_in.at[own, jn],
                       snap_send.at[q, d], snap_recv.at[q, jn], (iw, peer))
            )
        for copy in started:
            copy.start()
        return started

    offset = lax.rem(jn * z_own, LANES)
    spread = (
        lax.rem(lax.broadcasted_iota(jnp.int32, (y_all, LANES), 1), y_all)
        == lax.broadcasted_iota(jnp.int32, (y_all, LANES), 0)
    ).astype(jnp.bfloat16)
    z_id = lax.broadcasted_iota(jnp.int32, (LANES, LANES), 0) - offset
    k_id = lax.broadcasted_iota(jnp.int32, (LANES, LANES), 1) // y_all
    fits = lax.rem(z_id + LANES, z_group) == k_id
    pick_row = lax.broadcasted_iota(jnp.int32, (16 * groups, LANES), 0)
    pick_z = lax.broadcasted_iota(jnp.int32, (16 * groups, LANES), 1) - offset
    inside = (pick_z >= 0) & (pick_z // z_group == pick_row // 16)

    def order_snapshots(q):
        own, made = pl.ds(2 * q, 2), pl.ds(2 * q + 1, 2)
        for d in range(1, narrow):
            peer = n_peer(d)
            remote(packed.at[made, 0], snap_in.at[own, peer], snap_send.at[q, d], snap_recv.at[q, peer], (iw, peer)).wait_recv()
        arrived = [[snap_in[2 * q + i, n].astype(jnp.float32) for n in range(narrow)] for i in range(2)]
        pick = jnp.concatenate(
            [inside & (lax.rem(pick_row, 16) == 16 - stages + 2 * q + i) for i in range(2)], 1
        ).astype(jnp.bfloat16)
        for c in range(comps):
            chosen = []
            for i in range(2):
                cells = jnp.concatenate([a[c * cells_y : (c + 1) * cells_y, :] for a in arrived[i]], 0)
                wide_cells = lax.dot_general(
                    cells.astype(jnp.bfloat16), spread, (((0,), (0,)), ((), ())), preferred_element_type=jnp.float32
                )
                chosen.append(jnp.where(fits, wide_cells, 0.0).astype(jnp.bfloat16))
            ordered = jnp.dot(pick, jnp.concatenate(chosen, 0), preferred_element_type=jnp.float32)
            flat = jnp.concatenate([ordered[16 * g : 16 * g + 16, :] for g in range(groups)], 1)
            tail[c] = tail[c] + flat.astype(jnp.bfloat16)

    tiles, pivots = [], []
    inverse_cells = 1.0 / (wide * narrow * cells_y * cells_z)

    def begin():
        for t in range(columns // 8):
            rows = whole[(8 * t) // piece_rows, (8 * t) % piece_rows : (8 * t) % piece_rows + 8, :]
            tiles.append(rows * inverse_cells)

    def run(start, stop):
        for p in range(start, stop):
            pivots.append(eliminate_panel(tiles, p, 0, min(8, prior - 8 * p)))

    row = lax.broadcasted_iota(jnp.int32, (cells_y, cells_z), 0)

    def line(values, k):
        return [jnp.broadcast_to(v[k : k + 1, :], (cells_y, cells_z)) for v in values]

    def lines(ref):
        return [jnp.broadcast_to(ref[c : c + 1, :], (cells_y, cells_z)) for c in range(comps)]

    def either(low, high):
        return [jnp.where(row == 0, a, b) for a, b in zip(low, high)]

    def shifted(here, low, high):
        below = [jnp.where(row == 0, a, pltpu.roll(c, 1, 0)) for a, c in zip(low, here)]
        above = [
            jnp.where(row == cells_y - 1, a, pltpu.roll(c, cells_y - 1, 0)) for a, c in zip(high, here)
        ]
        return below, above

    def change_of(inner, x_low, x_high, y_low, y_high):
        return [a + b + c for a, b, c in zip(inner, along(x_low, x_high, 0), along(y_low, y_high, 1))]

    def moved(here, inner, x_low, x_high, y_low, y_high):
        change = change_of(inner, x_low, x_high, y_low, y_high)
        return [a + TIME_STEP * b for a, b in zip(here, change)]

    for q in range(STEPS):
        inner = inner_part(current)
        for copy in copies:
            copy.wait_recv()
        planes = [unpack(x_halo.at[q, side]) for side in range(4)]
        low, high = lines(y_halo.at[q, 0, 0]), lines(y_halo.at[q, 1, 0])
        corner = [[lines(d_halo.at[q, i, j]) for j in range(2)] for i in range(2)]
        first_own = moved(current, inner, planes[0], planes[1], *shifted(current, low, high))
        put_state(2 * q + 1, first_own)
        first_low = moved(
            planes[0], inner_part(planes[0]), planes[2], current, *shifted(planes[0], *corner[0])
        )
        first_high = moved(
            planes[1], inner_part(planes[1]), current, planes[3], *shifted(planes[1], *corner[1])
        )
        rim = either(low, high)
        first_rim = moved(
            rim, inner_part(rim), either(*corner[0]), either(*corner[1]),
            either(lines(y_halo.at[q, 0, 1]), line(current, cells_y - 1)),
            either(line(current, 0), lines(y_halo.at[q, 1, 1])),
        )
        second = moved(
            first_own, inner_part(first_own), first_low, first_high,
            *shifted(first_own, line(first_rim, 0), line(first_rim, 1)),
        )
        current = [0.5 * a + 0.5 * b for a, b in zip(current, second)]
        put_state(2 * q + 2, current)
        if q + 1 < STEPS:
            copies = halo_copies(q + 1)
            for copy in copies:
                copy.start()
            pending += copies
        pending += send_snapshots(q)
        if q == 0:
            pending += reduce_step(1)
            order_snapshots(0)
            pending += reduce_step(2)
    reduce_step(3)
    begin()
    run(0, 3)
    for c in range(comps):
        flow[c] = current[c]

    order_snapshots(STEPS - 1)
    total = jnp.zeros((columns, 16), jnp.float32)
    for c in range(comps):
        rows = tail[c]
        x = jnp.concatenate([modes[c, 0:keep, :], rows], 0)
        total = total + lax.dot_general(x, rows, NT, preferred_element_type=jnp.float32)
    mine8 = jnp.transpose(total)[8:16, :]
    rows8[...] = mine8
    rows_n[jn] = mine8
    started = [
        remote(rows8, rows_n.at[jn], last_send.at[0, d], last_recv.at[0, jn], (iw, n_peer(d)))
        for d in range(1, narrow)
    ]
    for copy in started:
        copy.start()
    pending += started
    run(3, 9)
    for d in range(1, narrow):
        peer = n_peer(d)
        remote(rows8, rows_n.at[peer], last_send.at[0, d], last_recv.at[0, peer], (iw, peer)).wait_recv()
    sum8 = rows_n[0]
    for n in range(1, narrow):
        sum8 = sum8 + rows_n[n]
    sums8[...] = sum8
    rows_w[iw] = sum8
    started = [
        remote(sums8, rows_w.at[iw], last_send.at[1, d], last_recv.at[1, iw], (w_peer(d), jn))
        for d in range(1, wide)
    ]
    for copy in started:
        copy.start()
    pending += started
    run(9, columns // 8)
    lane, row = lane_ids(), row_ids()
    uppers, inverse = [], []
    for t in range(columns // 8):
        scale = lax.rsqrt(jnp.where(pivots[t] > 0.0, pivots[t], 1.0))
        scale = jnp.where(row + 8 * t < prior, scale, 0.0)
        uppers.append(jnp.where(lane >= row + 8 * t, tiles[t], 0.0) * scale)
        left = jnp.where(lane < row + 8 * t, tiles[t], 0.0)
        inverse.append(jnp.where(lane == row + 8 * t, 1.0, left) * scale)
    inverse = jnp.concatenate(inverse, 0)
    for copy in pending:
        copy.wait_send()
    for d in range(1, wide):
        peer = w_peer(d)
        remote(sums8, rows_w.at[peer], last_send.at[1, d], last_recv.at[1, peer], (peer, jn)).wait_recv()
    sum8 = rows_w[0]
    for w in range(1, wide):
        sum8 = sum8 + rows_w[w]

    exact = lax.Precision.HIGHEST
    corner = row + columns - 8 >= prior
    rows = jnp.where(corner, sum8 * inverse_cells, 0.0)
    known = jnp.where(lane < prior, rows, 0.0)
    solved = lax.dot_general(known, inverse, NT, precision=exact, preferred_element_type=jnp.float32)
    bottom = jnp.concatenate([jnp.zeros((columns - 8, columns), jnp.float32), solved], 0)
    taken = lax.dot_general(solved, bottom, NT, precision=exact, preferred_element_type=jnp.float32)
    last_tile = [jnp.where(lane >= prior, rows - taken, 0.0)]
    last_tile = [pltpu.roll(last_tile[0], 8, 1)]
    left = eliminate_panel(last_tile, 0, prior - (columns - 8), 8)
    tip = jnp.where(lane >= row, last_tile[0], 0.0) * lax.rsqrt(jnp.where(corner, left, 1.0))
    tip = pltpu.roll(jnp.where(corner, tip, 0.0), LANES - 8, 1)
    side = jnp.transpose(bottom)
    for t in range(columns // 8):
        out = uppers[t] + side[8 * t : 8 * t + 8, :]
        if t == columns // 8 - 1:
            out = jnp.where(corner, tip, out)
        factor_out[8 * t : 8 * t + 8, :] = out


def local(wide, narrow, fields, prior_modes):
    comps, cells_x, cells_y, cells_z = fields.shape
    prior = prior_modes.shape[0]
    stages = 2 * STEPS
    columns = prior + stages
    modes = jnp.transpose(prior_modes, (1, 2, 0, 3)).reshape(comps, prior, prior_modes.shape[3])
    piece = columns // wide
    snap_rows = -(-comps * cells_y // 16) * 16
    f32, bf16 = jnp.float32, jnp.bfloat16
    vmem = pl.BlockSpec(memory_space=pltpu.VMEM)
    dma = pltpu.SemaphoreType.DMA
    flow, factor = pl.pallas_call(
        functools.partial(kernel, wide, narrow),
        out_shape=(
            jax.ShapeDtypeStruct((comps, cells_y, cells_z), f32),
            jax.ShapeDtypeStruct((columns, columns), f32),
        ),
        in_specs=[pl.BlockSpec(memory_space=pltpu.HBM)] * 2,
        out_specs=(vmem, vmem),
        scratch_shapes=[
            pltpu.VMEM(modes.shape, bf16), dma((comps,)),
            pltpu.VMEM((comps, cells_y, cells_z), f32), dma((1,)),
            pltpu.VMEM((stages + 1, cells_z // LANES, snap_rows, LANES), bf16),
            pltpu.VMEM((STEPS, 4, cells_z // LANES, snap_rows, LANES), bf16),
            pltpu.VMEM((STEPS, 2, 2, 8, cells_z), f32),
            pltpu.VMEM((STEPS, 2, 2, 8, cells_z), f32),
            pltpu.VMEM((STEPS, 2, 2, 8, cells_z), f32),
            dma((STEPS, 10)), dma((STEPS, 10)),
            pltpu.VMEM((stages, narrow, snap_rows, LANES), bf16),
            dma((STEPS, narrow)), dma((STEPS, narrow)),
            pltpu.VMEM((columns, columns), f32),
            pltpu.VMEM((wide, piece, columns), f32),
            pltpu.VMEM((piece, columns), f32),
            pltpu.VMEM((narrow, piece, columns), f32),
            pltpu.VMEM((wide, piece, columns), f32),
            pltpu.VMEM((piece, columns), f32),
            dma((3, max(wide, narrow))), dma((3, max(wide, narrow))),
            pltpu.VMEM((comps, 16, modes.shape[2]), bf16),
            pltpu.VMEM((8, columns), f32),
            pltpu.VMEM((narrow, 8, columns), f32),
            pltpu.VMEM((8, columns), f32),
            pltpu.VMEM((wide, 8, columns), f32),
            dma((2, max(wide, narrow))), dma((2, max(wide, narrow))),
        ],
        compiler_params=pltpu.CompilerParams(
            collective_id=0, has_side_effects=True, vmem_limit_bytes=52 * 1024 * 1024
        ),
    )(fields.reshape(comps, cells_y, cells_z), modes)
    return flow.reshape(fields.shape), factor


def solution(mesh):
    wide, narrow = mesh.shape["wide"], mesh.shape["narrow"]
    return jax.shard_map(
        functools.partial(local, wide, narrow),
        mesh=mesh,
        in_specs=(P(None, "wide", "narrow", None), P(None, None, "wide", "narrow")),
        out_specs=(P(None, "wide", "narrow", None), P()),
        check_vma=False,
    )
```

```python
import functools

import jax
import jax.numpy as jnp
from jax import lax
from jax.experimental import pallas as pl
from jax.experimental.pallas import tpu as pltpu
from jax.sharding import PartitionSpec as P

STEPS = 2
GAMMA = 1.4
TIME_STEP = 0.25
VISCOSITY = 0.15
LANES = 128
NT = (((1,), (1,)), ((), ()))


def flux_of(state, d):
    density, energy = state[0], state[4]
    momentum = state[1:4]
    inverse = 1.0 / density
    vel = momentum[d] * inverse
    squares = momentum[0] * momentum[0] + momentum[1] * momentum[1] + momentum[2] * momentum[2]
    pressure = (GAMMA - 1.0) * (energy - 0.5 * squares * inverse)
    out = [momentum[d], momentum[0] * vel, momentum[1] * vel, momentum[2] * vel]
    out.append((energy + pressure) * vel)
    out[1 + d] = out[1 + d] + pressure
    return out


def along(low, high, d):
    return [
        -0.5 * (fh - fl) + VISCOSITY * (l + h)
        for fh, fl, l, h in zip(flux_of(high, d), flux_of(low, d), low, high)
    ]


def inner_part(here):
    cells_z = here[0].shape[1]
    z_low = [pltpu.roll(c, 1, 1) for c in here]
    z_high = [pltpu.roll(c, cells_z - 1, 1) for c in here]
    return [a - (6.0 * VISCOSITY) * c for a, c in zip(along(z_low, z_high, 2), here)]


def lane_ids():
    return lax.broadcasted_iota(jnp.int32, (8, LANES), 1)


def row_ids():
    return lax.broadcasted_iota(jnp.int32, (8, LANES), 0)


def column_of(tile, j):
    return jnp.broadcast_to(tile[:, j : j + 1], (8, LANES))


def row_of(tile, k):
    return jnp.broadcast_to(tile[k : k + 1, :], (8, LANES))


def inverted(x):
    guess = pl.reciprocal(x, approx=True)
    guess = guess * (2.0 - x * guess)
    return guess * (2.0 - x * guess)


def eliminate_panel(tiles, p, first, last):
    lane, row = lane_ids(), row_ids()
    steps = range(first, last)
    panel = tiles[p]
    inside = (lane >= 8 * p + first) & (lane < 8 * p + last)
    spread = {k: column_of(panel, 8 * p + k) for k in steps}
    entry = {(m, k): row_of(spread[k], m) for k in steps for m in range(k, last)}
    inverses, ratio = {}, {}
    for k in steps:
        inverses[k] = inverted(entry[k, k])
        for m in range(k + 1, last):
            ratio[m, k] = entry[m, k] * inverses[k]
            for n in range(m, last):
                entry[n, m] = entry[n, m] - entry[n, k] * ratio[m, k]
    raw = {k: row_of(panel, k) for k in steps}
    heads = {k: jnp.where(inside, jnp.where(lane == 8 * p + k, 1.0, 0.0), raw[k]) for k in steps}
    for k in steps:
        for m in range(first, k):
            raw[k] = raw[k] - ratio[k, m] * raw[m]
            heads[k] = heads[k] - ratio[k, m] * heads[m]
    pivots = jnp.zeros((8, LANES), jnp.float32)
    panel = jnp.zeros((8, LANES), jnp.float32)
    for k in steps:
        pivots = jnp.where(row == k, entry[k, k], pivots)
        panel = jnp.where(row == k, jnp.where(inside & (lane < 8 * p + k), heads[k], raw[k]), panel)
    tiles[p] = panel
    for t in range(p + 1, len(tiles)):
        rest = jnp.where(inside, 0.0, tiles[t])
        factors = {}
        for k in steps:
            left = column_of(tiles[t], 8 * p + k)
            for m in range(first, k):
                left = left - factors[m] * entry[k, m]
            factors[k] = left * inverses[k]
            rest = rest - factors[k] * heads[k]
        tiles[t] = rest
    return pivots


def kernel(
    wide, narrow, fields, modes_hbm, flow, factor_out,
    modes, modes_sem, start, start_sem, packed, x_halo, y_send, y_halo, d_halo, halo_send, halo_recv,
    snap_in, snap_send, snap_recv,
    gram, scatter, part, share, whole, piece, red_send, red_recv,
    tail, rows8, rows_n, sums8, rows_w, last_send, last_recv,
):
    stages = 2 * STEPS
    comps, cells_y, cells_z = fields.shape
    prior = modes.shape[1]
    columns = gram.shape[0]
    mode_lanes = modes.shape[2]
    y_all = cells_y * narrow
    z_own = cells_z // narrow
    z_group = LANES // y_all
    groups = mode_lanes // LANES
    piece_rows = columns // wide
    keep = columns - 16
    iw, jn = lax.axis_index("wide"), lax.axis_index("narrow")

    w_peers = [lax.rem(iw + d, wide) for d in range(wide)]
    n_peers = [lax.rem(jn + d, narrow) for d in range(narrow)]

    def w_peer(d):
        return w_peers[d % wide]

    def n_peer(d):
        return n_peers[d % narrow]

    def remote(src, dst, send, recv, device):
        return pltpu.make_async_remote_copy(
            src_ref=src, dst_ref=dst, send_sem=send, recv_sem=recv,
            device_id=device, device_id_type=pl.DeviceIdType.MESH,
        )

    loads = [pltpu.make_async_copy(modes_hbm.at[c], modes.at[c], modes_sem.at[c]) for c in range(comps)]
    fields_load = pltpu.make_async_copy(fields, start, start_sem.at[0])
    fields_load.start()
    for load in loads:
        load.start()

    barrier = pltpu.get_barrier_semaphore()
    for d in range(1, wide):
        pl.semaphore_signal(barrier, inc=1, device_id=(w_peer(d), jn), device_id_type=pl.DeviceIdType.MESH)
    for d in range(1, narrow):
        pl.semaphore_signal(barrier, inc=1, device_id=(iw, n_peer(d)), device_id_type=pl.DeviceIdType.MESH)

    for d in (1, wide - 1):
        for e in (1, narrow - 1):
            pl.semaphore_signal(barrier, inc=1, device_id=(w_peer(d), n_peer(e)), device_id_type=pl.DeviceIdType.MESH)

    def halo_copies(q):
        moves = []
        for side, d in enumerate((1, -1, 2, -2)):
            moves.append((packed.at[2 * q], x_halo.at[q, side], (w_peer(d), jn)))
        for e, y_side in ((1, 0), (-1, 1)):
            moves.append((y_send.at[q, 1 - y_side], y_halo.at[q, y_side], (iw, n_peer(e))))
            for d, x_side in ((1, 0), (-1, 1)):
                moves.append((y_send.at[q, 1 - y_side, 0], d_halo.at[q, x_side, y_side], (w_peer(d), n_peer(e))))
        return [
            remote(src, dst, halo_send.at[q, i], halo_recv.at[q, i], device)
            for i, (src, dst, device) in enumerate(moves)
        ]

    def put_state(s, values):
        spare = jnp.zeros((packed.shape[2] - comps * cells_y, cells_z), jnp.float32)
        stacked = jnp.concatenate(values + [spare], 0).astype(jnp.bfloat16)
        for b in range(cells_z // LANES):
            packed[s, b] = stacked[:, b * LANES : (b + 1) * LANES]
        if s % 2 == 0 and s < stages:
            for depth in range(2):
                for c in range(comps):
                    y_send[s // 2, 0, depth, c : c + 1, :] = values[c][depth : depth + 1, :]
                    top = cells_y - 1 - depth
                    y_send[s // 2, 1, depth, c : c + 1, :] = values[c][top : top + 1, :]
                for c in range(comps, 8):
                    y_send[s // 2, 0, depth, c : c + 1, :] = jnp.zeros((1, cells_z), jnp.float32)
                    y_send[s // 2, 1, depth, c : c + 1, :] = jnp.zeros((1, cells_z), jnp.float32)

    def unpack(ref):
        blocks = [ref[b].astype(jnp.float32) for b in range(cells_z // LANES)]
        return [
            jnp.concatenate([x[c * cells_y : (c + 1) * cells_y, :] for x in blocks], 1)
            for c in range(comps)
        ]

    fields_load.wait()
    current = [start[c] for c in range(comps)]
    put_state(0, current)
    def gram_part(c):
        loads[c].wait()
        last = modes[c, keep:prior, :].astype(jnp.float32)
        last = jnp.concatenate([last, jnp.zeros((columns - prior, mode_lanes), jnp.float32)], 0)
        tail[c] = last.astype(jnp.bfloat16)
        x = jnp.concatenate([modes[c, 0:keep, :], tail[c]], 0)
        return lax.dot_general(x, x, NT, preferred_element_type=jnp.float32)

    early = comps // 2 + 1
    total = gram_part(0)
    for c in range(1, early):
        total = total + gram_part(c)
    pl.semaphore_wait(barrier, wide + narrow + 2)

    copies = halo_copies(0)
    for copy in copies:
        copy.start()
    pending = list(copies)

    for c in range(early, comps):
        total = total + gram_part(c)
    gram[...] = total
    mine = pl.ds(pl.multiple_of(iw * piece_rows, piece_rows), piece_rows)
    scatter[iw] = gram[mine, :]
    first = []
    for d in range(1, wide):
        peer = w_peer(d)
        theirs = pl.ds(pl.multiple_of(peer * piece_rows, piece_rows), piece_rows)
        first.append(remote(gram.at[theirs], scatter.at[iw], red_send.at[0, d], red_recv.at[0, iw], (peer, jn)))
    for copy in first:
        copy.start()
    pending += first

    def reduce_step(s):
        started = []
        if s == 1:
            for d in range(1, wide):
                peer = w_peer(d)
                remote(gram.at[mine], scatter.at[peer], red_send.at[0, d], red_recv.at[0, peer], (peer, jn)).wait_recv()
            acc = scatter[0]
            for w in range(1, wide):
                acc = acc + scatter[w]
            part[...] = acc
            share[jn] = acc
            for d in range(1, narrow):
                started.append(remote(part, share.at[jn], red_send.at[1, d], red_recv.at[1, jn], (iw, n_peer(d))))
        elif s == 2:
            for d in range(1, narrow):
                peer = n_peer(d)
                remote(part, share.at[peer], red_send.at[1, d], red_recv.at[1, peer], (iw, peer)).wait_recv()
            acc = share[0]
            for n in range(1, narrow):
                acc = acc + share[n]
            piece[...] = acc
            whole[iw] = acc
            for d in range(1, wide):
                started.append(remote(piece, whole.at[iw], red_send.at[2, d], red_recv.at[2, iw], (w_peer(d), jn)))
        elif s == 3:
            for d in range(1, wide):
                peer = w_peer(d)
                remote(piece, whole.at[peer], red_send.at[2, d], red_recv.at[2, peer], (peer, jn)).wait_recv()
        for copy in started:
            copy.start()
        return started

    def send_snapshots(q):
        own, made = pl.ds(2 * q, 2), pl.ds(2 * q + 1, 2)
        for i in range(2):
            snap_in[2 * q + i, jn] = packed[2 * q + 1 + i, (jn * z_own) // LANES]
        started = []
        for d in range(1, narrow):
            peer = n_peer(d)
            started.append(
                remote(packed.at[made, (peer * z_own) // LANES], snap_in.at[own, jn],
                       snap_send.at[q, d], snap_recv.at[q, jn], (iw, peer))
            )
        for copy in started:
            copy.start()
        return started

    offset = lax.rem(jn * z_own, LANES)
    spread = (
        lax.rem(lax.broadcasted_iota(jnp.int32, (y_all, LANES), 1), y_all)
        == lax.broadcasted_iota(jnp.int32, (y_all, LANES), 0)
    ).astype(jnp.bfloat16)
    z_id = lax.broadcasted_iota(jnp.int32, (LANES, LANES), 0) - offset
    k_id = lax.broadcasted_iota(jnp.int32, (LANES, LANES), 1) // y_all
    fits = lax.rem(z_id + LANES, z_group) == k_id
    pick_row = lax.broadcasted_iota(jnp.int32, (16 * groups, LANES), 0)
    pick_z = lax.broadcasted_iota(jnp.int32, (16 * groups, LANES), 1) - offset
    inside = (pick_z >= 0) & (pick_z // z_group == pick_row // 16)

    def order_snapshots(q):
        own, made = pl.ds(2 * q, 2), pl.ds(2 * q + 1, 2)
        for d in range(1, narrow):
            peer = n_peer(d)
            remote(packed.at[made, 0], snap_in.at[own, peer], snap_send.at[q, d], snap_recv.at[q, peer], (iw, peer)).wait_recv()
        arrived = [[snap_in[2 * q + i, n].astype(jnp.float32) for n in range(narrow)] for i in range(2)]
        pick = jnp.concatenate(
            [inside & (lax.rem(pick_row, 16) == 16 - stages + 2 * q + i) for i in range(2)], 1
        ).astype(jnp.bfloat16)
        for c in range(comps):
            chosen = []
            for i in range(2):
                cells = jnp.concatenate([a[c * cells_y : (c + 1) * cells_y, :] for a in arrived[i]], 0)
                wide_cells = lax.dot_general(
                    cells.astype(jnp.bfloat16), spread, (((0,), (0,)), ((), ())), preferred_element_type=jnp.float32
                )
                chosen.append(jnp.where(fits, wide_cells, 0.0).astype(jnp.bfloat16))
            ordered = jnp.dot(pick, jnp.concatenate(chosen, 0), preferred_element_type=jnp.float32)
            flat = jnp.concatenate([ordered[16 * g : 16 * g + 16, :] for g in range(groups)], 1)
            tail[c] = tail[c] + flat.astype(jnp.bfloat16)

    tiles, pivots = [], []
    inverse_cells = 1.0 / (wide * narrow * cells_y * cells_z)

    def begin():
        for t in range(columns // 8):
            rows = whole[(8 * t) // piece_rows, (8 * t) % piece_rows : (8 * t) % piece_rows + 8, :]
            tiles.append(rows * inverse_cells)

    def run(start, stop):
        for p in range(start, stop):
            pivots.append(eliminate_panel(tiles, p, 0, min(8, prior - 8 * p)))

    row = lax.broadcasted_iota(jnp.int32, (cells_y, cells_z), 0)

    def line(values, k):
        return [jnp.broadcast_to(v[k : k + 1, :], (cells_y, cells_z)) for v in values]

    def lines(ref):
        return [jnp.broadcast_to(ref[c : c + 1, :], (cells_y, cells_z)) for c in range(comps)]

    def either(low, high):
        return [jnp.where(row == 0, a, b) for a, b in zip(low, high)]

    def shifted(here, low, high):
        below = [jnp.where(row == 0, a, pltpu.roll(c, 1, 0)) for a, c in zip(low, here)]
        above = [
            jnp.where(row == cells_y - 1, a, pltpu.roll(c, cells_y - 1, 0)) for a, c in zip(high, here)
        ]
        return below, above

    def change_of(inner, x_low, x_high, y_low, y_high):
        return [a + b + c for a, b, c in zip(inner, along(x_low, x_high, 0), along(y_low, y_high, 1))]

    def moved(here, inner, x_low, x_high, y_low, y_high):
        change = change_of(inner, x_low, x_high, y_low, y_high)
        return [a + TIME_STEP * b for a, b in zip(here, change)]

    for q in range(STEPS):
        inner = inner_part(current)
        for copy in copies:
            copy.wait_recv()
        planes = [unpack(x_halo.at[q, side]) for side in range(4)]
        low, high = lines(y_halo.at[q, 0, 0]), lines(y_halo.at[q, 1, 0])
        corner = [[lines(d_halo.at[q, i, j]) for j in range(2)] for i in range(2)]
        first_own = moved(current, inner, planes[0], planes[1], *shifted(current, low, high))
        put_state(2 * q + 1, first_own)
        first_low = moved(
            planes[0], inner_part(planes[0]), planes[2], current, *shifted(planes[0], *corner[0])
        )
        first_high = moved(
            planes[1], inner_part(planes[1]), current, planes[3], *shifted(planes[1], *corner[1])
        )
        rim = either(low, high)
        first_rim = moved(
            rim, inner_part(rim), either(*corner[0]), either(*corner[1]),
            either(lines(y_halo.at[q, 0, 1]), line(current, cells_y - 1)),
            either(line(current, 0), lines(y_halo.at[q, 1, 1])),
        )
        second = moved(
            first_own, inner_part(first_own), first_low, first_high,
            *shifted(first_own, line(first_rim, 0), line(first_rim, 1)),
        )
        current = [0.5 * a + 0.5 * b for a, b in zip(current, second)]
        put_state(2 * q + 2, current)
        if q + 1 < STEPS:
            copies = halo_copies(q + 1)
            for copy in copies:
                copy.start()
            pending += copies
        pending += send_snapshots(q)
        if q == 0:
            pending += reduce_step(1)
            order_snapshots(0)
            pending += reduce_step(2)
    reduce_step(3)
    begin()
    run(0, 3)
    for c in range(comps):
        flow[c] = current[c]

    order_snapshots(STEPS - 1)
    total = jnp.zeros((columns, 16), jnp.float32)
    for c in range(comps):
        rows = tail[c]
        x = jnp.concatenate([modes[c, 0:keep, :], rows], 0)
        total = total + lax.dot_general(x, rows, NT, preferred_element_type=jnp.float32)
    mine8 = jnp.transpose(total)[8:16, :]
    rows8[...] = mine8
    rows_n[jn] = mine8
    started = [
        remote(rows8, rows_n.at[jn], last_send.at[0, d], last_recv.at[0, jn], (iw, n_peer(d)))
        for d in range(1, narrow)
    ]
    for copy in started:
        copy.start()
    pending += started
    run(3, 9)
    for d in range(1, narrow):
        peer = n_peer(d)
        remote(rows8, rows_n.at[peer], last_send.at[0, d], last_recv.at[0, peer], (iw, peer)).wait_recv()
    sum8 = rows_n[0]
    for n in range(1, narrow):
        sum8 = sum8 + rows_n[n]
    sums8[...] = sum8
    rows_w[iw] = sum8
    started = [
        remote(sums8, rows_w.at[iw], last_send.at[1, d], last_recv.at[1, iw], (w_peer(d), jn))
        for d in range(1, wide)
    ]
    for copy in started:
        copy.start()
    pending += started
    run(9, columns // 8)
    lane, row = lane_ids(), row_ids()
    uppers, inverse = [], []
    for t in range(columns // 8):
        scale = lax.rsqrt(jnp.where(pivots[t] > 0.0, pivots[t], 1.0))
        scale = jnp.where(row + 8 * t < prior, scale, 0.0)
        uppers.append(jnp.where(lane >= row + 8 * t, tiles[t], 0.0) * scale)
        left = jnp.where(lane < row + 8 * t, tiles[t], 0.0)
        inverse.append(jnp.where(lane == row + 8 * t, 1.0, left) * scale)
    inverse = jnp.concatenate(inverse, 0)
    for copy in pending:
        copy.wait_send()
    for d in range(1, wide):
        peer = w_peer(d)
        remote(sums8, rows_w.at[peer], last_send.at[1, d], last_recv.at[1, peer], (peer, jn)).wait_recv()
    sum8 = rows_w[0]
    for w in range(1, wide):
        sum8 = sum8 + rows_w[w]

    exact = lax.Precision.HIGHEST
    corner = row + columns - 8 >= prior
    rows = jnp.where(corner, sum8 * inverse_cells, 0.0)
    known = jnp.where(lane < prior, rows, 0.0)
    solved = lax.dot_general(known, inverse, NT, precision=exact, preferred_element_type=jnp.float32)
    bottom = jnp.concatenate([jnp.zeros((columns - 8, columns), jnp.float32), solved], 0)
    taken = lax.dot_general(solved, bottom, NT, precision=exact, preferred_element_type=jnp.float32)
    last_tile = [jnp.where(lane >= prior, rows - taken, 0.0)]
    last_tile = [pltpu.roll(last_tile[0], 8, 1)]
    left = eliminate_panel(last_tile, 0, prior - (columns - 8), 8)
    tip = jnp.where(lane >= row, last_tile[0], 0.0) * lax.rsqrt(jnp.where(corner, left, 1.0))
    tip = pltpu.roll(jnp.where(corner, tip, 0.0), LANES - 8, 1)
    side = jnp.transpose(bottom)
    for t in range(columns // 8):
        out = uppers[t] + side[8 * t : 8 * t + 8, :]
        if t == columns // 8 - 1:
            out = jnp.where(corner, tip, out)
        factor_out[8 * t : 8 * t + 8, :] = out


def local(wide, narrow, fields, prior_modes):
    comps, cells_x, cells_y, cells_z = fields.shape
    prior = prior_modes.shape[0]
    stages = 2 * STEPS
    columns = prior + stages
    modes = jnp.transpose(prior_modes, (1, 2, 0, 3)).reshape(comps, prior, prior_modes.shape[3])
    piece = columns // wide
    snap_rows = -(-comps * cells_y // 16) * 16
    f32, bf16 = jnp.float32, jnp.bfloat16
    vmem = pl.BlockSpec(memory_space=pltpu.VMEM)
    dma = pltpu.SemaphoreType.DMA
    flow, factor = pl.pallas_call(
        functools.partial(kernel, wide, narrow),
        out_shape=(
            jax.ShapeDtypeStruct((comps, cells_y, cells_z), f32),
            jax.ShapeDtypeStruct((columns, columns), f32),
        ),
        in_specs=[pl.BlockSpec(memory_space=pltpu.HBM)] * 2,
        out_specs=(vmem, vmem),
        scratch_shapes=[
            pltpu.VMEM(modes.shape, bf16), dma((comps,)),
            pltpu.VMEM((comps, cells_y, cells_z), f32), dma((1,)),
            pltpu.VMEM((stages + 1, cells_z // LANES, snap_rows, LANES), bf16),
            pltpu.VMEM((STEPS, 4, cells_z // LANES, snap_rows, LANES), bf16),
            pltpu.VMEM((STEPS, 2, 2, 8, cells_z), f32),
            pltpu.VMEM((STEPS, 2, 2, 8, cells_z), f32),
            pltpu.VMEM((STEPS, 2, 2, 8, cells_z), f32),
            dma((STEPS, 10)), dma((STEPS, 10)),
            pltpu.VMEM((stages, narrow, snap_rows, LANES), bf16),
            dma((STEPS, narrow)), dma((STEPS, narrow)),
            pltpu.VMEM((columns, columns), f32),
            pltpu.VMEM((wide, piece, columns), f32),
            pltpu.VMEM((piece, columns), f32),
            pltpu.VMEM((narrow, piece, columns), f32),
            pltpu.VMEM((wide, piece, columns), f32),
            pltpu.VMEM((piece, columns), f32),
            dma((3, max(wide, narrow))), dma((3, max(wide, narrow))),
            pltpu.VMEM((comps, 16, modes.shape[2]), bf16),
            pltpu.VMEM((8, columns), f32),
            pltpu.VMEM((narrow, 8, columns), f32),
            pltpu.VMEM((8, columns), f32),
            pltpu.VMEM((wide, 8, columns), f32),
            dma((2, max(wide, narrow))), dma((2, max(wide, narrow))),
        ],
        compiler_params=pltpu.CompilerParams(
            collective_id=0, has_side_effects=True, vmem_limit_bytes=52 * 1024 * 1024
        ),
    )(fields.reshape(comps, cells_y, cells_z), modes)
    return flow.reshape(fields.shape), factor


def solution(mesh):
    wide, narrow = mesh.shape["wide"], mesh.shape["narrow"]
    return jax.shard_map(
        functools.partial(local, wide, narrow),
        mesh=mesh,
        in_specs=(P(None, "wide", "narrow", None), P(None, None, "wide", "narrow")),
        out_specs=(P(None, "wide", "narrow", None), P()),
        check_vma=False,
    )
```
